256 devices in a mesh: gx: 16 (over x, z_hi, core), gy: 4 (over y), gz: 4 (over z_lo).
Axes of the slice: x: 4, y: 4, z: 8 (z_hi: 2, z_lo: 4; z = z_hi * 4 + z_lo), core: 2. Of those that a mesh axis runs over, the one named last changes fastest.
Arguments:
- fine_state: bfloat16 [262144, 512], P(('gx', 'gy', 'gz')), may hold values from -6 to 6
- fine_nbrs: int32 [262144, 6], P(('gx', 'gy', 'gz')), may hold values from 0 to 1792, as said below
- send_rows: int32 [256, 6, 128], P(('gx', 'gy', 'gz')), may hold values from 0 to 1023
- ghost_counts: int32 [256, 6], P(('gx', 'gy', 'gz')), may hold values from 32 to 128, as said below
- fine_parent: int32 [262144], P(('gx', 'gy', 'gz')), may hold values from 0 to 127, as said below
- medium_state: bfloat16 [32768, 512], P(('gx', 'gy', 'gz')), may hold values from -6 to 6
- medium_parent: int32 [32768], P(('gx', 'gy', 'gz')), may hold values from 0 to 15, as said below
- coarse_state: bfloat16 [4096, 512], P(('gx', 'gy', 'gz')), may hold values from -6 to 6
- coarse_nbrs: int32 [4096, 64], P(('gx', 'gy', 'gz')), may hold values from 0 to 4095, as said below
- fine_edge_in: bfloat16 [1024, 512], replicated, may hold values from -0.1875 to 0.1875
- fine_edge_bias: float32 [512], replicated, may hold values from -3 to 3
- fine_edge_out: bfloat16 [512, 512], replicated, may hold values from -0.25 to 0.25
- fine_edge_gain: float32 [512], replicated, may hold values from 0.1 to 1.9
- fine_node_in: bfloat16 [1024, 512], replicated, may hold values from -0.1875 to 0.1875
- fine_node_bias: float32 [512], replicated, may hold values from -3 to 3
- fine_node_out: bfloat16 [512, 512], replicated, may hold values from -0.25 to 0.25
- fine_node_gain: float32 [512], replicated, may hold values from 0.1 to 1.9
- coarse_edge_in: bfloat16 [1024, 512], replicated, may hold values from -0.1875 to 0.1875
- coarse_edge_bias: float32 [512], replicated, may hold values from -3 to 3
- coarse_edge_out: bfloat16 [512, 512], replicated, may hold values from -0.25 to 0.25
- coarse_edge_gain: float32 [512], replicated, may hold values from 0.1 to 1.9
- coarse_node_in: bfloat16 [1024, 512], replicated, may hold values from -0.1875 to 0.1875
- coarse_node_bias: float32 [512], replicated, may hold values from -3 to 3
- coarse_node_out: bfloat16 [512, 512], replicated, may hold values from -0.25 to 0.25
- coarse_node_gain: float32 [512], replicated, may hold values from 0.1 to 1.9
Outputs:
- fine_out: bfloat16 [262144, 512], P(('gx', 'gy', 'gz'))
- medium_out: bfloat16 [32768, 512], P(('gx', 'gy', 'gz'))
- coarse_out: bfloat16 [4096, 512], P(('gx', 'gy', 'gz'))
The draws below stay inside these ranges and needn't reach their ends.
Inputs may be any that keep to these rules, and one draw needn't show every extreme that they name: `fine_nbrs`: row i of device p lists node i's neighbours as rows of table_p: 0 to 1023 own nodes, then 6 ghost blocks of 128 rows in the order of ghosts; a ghost row is named only if the sending neighbour exists and the row lies below that neighbour's count for the face it sends. The value 1024 + 6 * 128 marks an empty slot; empty slots follow the used ones, and at least 4 slots of every row are used. `ghost_counts`: entry f of device p counts the used rows of the block that p sends from face f; on every device one face is full. `send_rows`: local fine rows of the sending device; rows at or past the face's count are not used. `fine_parent`: A local medium index of the same device; every medium node has at least one child. `medium_parent`: A local coarse index of the same device; every coarse node has at least one child. `coarse_nbrs`: global coarse rows anywhere on the mesh.
All inputs are finite; a program needn't handle non-finite values.
Results may differ from the reference program's by a relative error of at most 0.0075.
Values may be sent and summed in bfloat16 or wider, within the bound.
No kernel may reach another device: no remote copies, remote signals or barrier semaphores. Data moves between devices by JAX's collectives and lax.ppermute only.
A program may use at most 128 MiB of HBM per device.

```python
import jax
import jax.numpy as jnp
from jax import lax

D = 512
K = 6
KC = 64
NF_DEV = 1024
G = 128
NM_DEV = 128
NC_DEV = 16
GRID_X = 16
GRID_Y = 4
GRID_Z = 4
NF = 262144
NM = 32768
NC = 4096
DEVICES = 256


def ghost_totals(key):
    base_counts = jax.random.randint(jax.random.fold_in(key, 11), (DEVICES, 6), G // 4, G + 1)
    full_face = jax.random.randint(jax.random.fold_in(key, 12), (DEVICES, 1), 0, 6)
    return jnp.where(jnp.arange(6)[None, :] == full_face, G, base_counts).astype(jnp.int32)


def draw_ghost_counts(key, part):
    return ghost_totals(key)


def draw_fine_nbrs(key, part):
    totals = ghost_totals(key)
    device = jnp.arange(DEVICES, dtype=jnp.int32)
    coords = (device // (GRID_Y * GRID_Z), device // GRID_Z % GRID_Y, device % GRID_Z)
    grid_sizes = (GRID_X, GRID_Y, GRID_Z)
    strides = (GRID_Y * GRID_Z, GRID_Z, 1)
    columns = []
    for axis_pos in range(3):
        lower_ok = coords[axis_pos] > 0
        upper_ok = coords[axis_pos] < grid_sizes[axis_pos] - 1
        lower_source = jnp.clip(device - strides[axis_pos], 0, DEVICES - 1)
        upper_source = jnp.clip(device + strides[axis_pos], 0, DEVICES - 1)
        columns.append(jnp.where(lower_ok, totals[lower_source, 2 * axis_pos + 1], 0))
        columns.append(jnp.where(upper_ok, totals[upper_source, 2 * axis_pos], 0))
    available = jnp.stack(columns, axis=1)
    device_keys = jax.random.split(jax.random.fold_in(key, 21), DEVICES)
    orders = jax.vmap(lambda one_key: jax.random.permutation(one_key, NF_DEV))(device_keys)
    ranks = jnp.argsort(orders, axis=1).astype(jnp.int32)
    block_index = jnp.minimum(ranks // G, 5)
    within = ranks % G
    limit_rows = jnp.take_along_axis(available, block_index, axis=1)
    ghost_ok = (ranks < 6 * G) & (within < limit_rows)
    local_picks = jax.random.randint(jax.random.fold_in(key, 22), (DEVICES, NF_DEV, K), 0, NF_DEV)
    degree = jax.random.randint(jax.random.fold_in(key, 23), (DEVICES, NF_DEV, 1), 4, K + 1)
    first_slot = jnp.where(ghost_ok, NF_DEV + ranks, local_picks[:, :, 0])
    neighbour_lists = jnp.concatenate([first_slot[:, :, None], local_picks[:, :, 1:]], axis=2)
    slot_index = jnp.arange(K, dtype=jnp.int32)[None, None, :]
    neighbour_lists = jnp.where(slot_index < degree, neighbour_lists, NF_DEV + 6 * G)
    return neighbour_lists.reshape(DEVICES * NF_DEV, K).astype(jnp.int32)


def parent_map(key, salt, children, parents):
    device_keys = jax.random.split(jax.random.fold_in(key, salt), DEVICES)
    orders = jax.vmap(lambda one_key: jax.random.permutation(one_key, children))(device_keys)
    random_parent = jax.random.randint(jax.random.fold_in(key, salt + 1), (DEVICES, children), 0, parents)
    return jnp.where(orders < parents, orders, random_parent).reshape(-1).astype(jnp.int32)


def draw_fine_parent(key, part):
    return parent_map(key, 31, NF_DEV, NM_DEV)


def draw_medium_parent(key, part):
    return parent_map(key, 41, NM_DEV, NC_DEV)


def draw_coarse_nbrs(key, part):
    anywhere = jax.random.randint(jax.random.fold_in(key, 51), (NC, KC), 0, NC)
    owner = jnp.arange(NC, dtype=jnp.int32) // NC_DEV
    far_owner = (owner + DEVICES // 2) % DEVICES
    far_rows = far_owner[:, None] * NC_DEV + jax.random.randint(jax.random.fold_in(key, 52), (NC, KC), 0, NC_DEV)
    slot_index = jnp.arange(KC, dtype=jnp.int32)[None, :]
    return jnp.where(slot_index < KC // 4, far_rows, anywhere).astype(jnp.int32)


def place_ends(result, own_key, smallest, high):
    dims = result.shape
    place = [jax.random.randint(jax.random.fold_in(own_key, axis), (), 0, dims[axis]) for axis in range(len(dims))]
    result = result.at[tuple(place)].set(smallest)
    longest = dims.index(max(dims))
    place[longest] = (place[longest] + 1) % dims[longest]
    return result.at[tuple(place)].set(high)


def shard_levels(rng, shape, shards, low, largest):
    loudness = 1.0
    for axis_at, shards_of in shards:
        steps = jax.random.uniform(jax.random.fold_in(jax.random.fold_in(rng, 6), axis_at), (shards_of,), jnp.float32, low / len(shards), largest / len(shards))
        loudness = loudness * jnp.repeat(jnp.exp(steps), shape[axis_at] // shards_of).reshape((-1,) + (1,) * (len(shape) - 1 - axis_at))
    return loudness


def scatter_about(own_key, shape, scale, limit, pieces=(), held_as=jnp.bfloat16):
    entries = scale * jax.random.normal(own_key, shape, jnp.float32)
    if pieces:
        entries = entries * shard_levels(own_key, shape, pieces, -0.22, 0.18)
    return jnp.clip(entries, -limit, limit).astype(held_as)


def setup_inputs(seed: int = 0) -> dict:
    streams_of = jax.random.split(jax.random.key(seed), 26)
    return {
        "fine_state": scatter_about(streams_of[0], (NF, D), 1.0, 6.0, ((0, 256),)),
        "fine_nbrs": draw_fine_nbrs(jax.random.fold_in(streams_of[25], 71), 0),
        "send_rows": place_ends(jax.random.randint(streams_of[2], (DEVICES, 6, G), 0, NF_DEV), jax.random.fold_in(streams_of[2], 1), 0, NF_DEV - 1).astype(jnp.int32),
        "ghost_counts": draw_ghost_counts(jax.random.fold_in(streams_of[25], 71), 0),
        "fine_parent": draw_fine_parent(jax.random.fold_in(streams_of[25], 71), 0),
        "medium_state": scatter_about(streams_of[5], (NM, D), 1.0, 6.0, ((0, 256),)),
        "medium_parent": draw_medium_parent(jax.random.fold_in(streams_of[25], 71), 0),
        "coarse_state": scatter_about(streams_of[7], (NC, D), 1.0, 6.0, ((0, 256),)),
        "coarse_nbrs": draw_coarse_nbrs(jax.random.fold_in(streams_of[25], 71), 0),
        "fine_edge_in": scatter_about(streams_of[9], (2 * D, D), (2 * D) ** -0.5, 0.1875),
        "fine_edge_bias": scatter_about(streams_of[10], (D,), 0.5, 3.0, (), jnp.float32),
        "fine_edge_out": scatter_about(streams_of[11], (D, D), D ** -0.5, 0.25),
        "fine_edge_gain": jnp.clip(1.0 + 0.18 * jax.random.normal(streams_of[12], (D,), jnp.float32), 0.1, 1.9),
        "fine_node_in": scatter_about(streams_of[13], (2 * D, D), (2 * D) ** -0.5, 0.1875),
        "fine_node_bias": scatter_about(streams_of[14], (D,), 0.5, 3.0, (), jnp.float32),
        "fine_node_out": scatter_about(streams_of[15], (D, D), D ** -0.5, 0.25),
        "fine_node_gain": jnp.clip(1.0 + 0.18 * jax.random.normal(streams_of[16], (D,), jnp.float32), 0.1, 1.9),
        "coarse_edge_in": scatter_about(streams_of[17], (2 * D, D), (2 * D) ** -0.5, 0.1875),
        "coarse_edge_bias": scatter_about(streams_of[18], (D,), 0.5, 3.0, (), jnp.float32),
        "coarse_edge_out": scatter_about(streams_of[19], (D, D), D ** -0.5, 0.25),
        "coarse_edge_gain": jnp.clip(1.0 + 0.18 * jax.random.normal(streams_of[20], (D,), jnp.float32), 0.1, 1.9),
        "coarse_node_in": scatter_about(streams_of[21], (2 * D, D), (2 * D) ** -0.5, 0.1875),
        "coarse_node_bias": scatter_about(streams_of[22], (D,), 0.5, 3.0, (), jnp.float32),
        "coarse_node_out": scatter_about(streams_of[23], (D, D), D ** -0.5, 0.25),
        "coarse_node_gain": jnp.clip(1.0 + 0.18 * jax.random.normal(streams_of[24], (D,), jnp.float32), 0.1, 1.9),
    }


def layer_norm(values):
    center = values - lax.optimization_barrier(jnp.mean(values, axis=-1, keepdims=True))
    spread = lax.optimization_barrier(jnp.mean(center * center, axis=-1, keepdims=True))
    return center * lax.rsqrt(spread + 1e-05)

def edge_messages(sender_rows, receiver, biases, out_weight, gains, slot_count):
    features = receiver.shape[1]
    combined = sender_rows.astype(jnp.float32).reshape(-1, slot_count, features) + receiver[:, None, :] + biases
    hidden = jax.nn.relu(combined).astype(jnp.bfloat16).reshape(-1, features)
    return layer_norm(jnp.dot(hidden, out_weight, preferred_element_type=jnp.float32)) * gains

def node_update(current, incoming, in_weight, biases, out_weight, gains):
    features = current.shape[1]
    combined = jnp.dot(current, in_weight[:features], preferred_element_type=jnp.float32)
    combined = combined + jnp.dot(incoming, in_weight[features:], preferred_element_type=jnp.float32) + biases
    hidden = jax.nn.relu(combined).astype(jnp.bfloat16)
    return layer_norm(jnp.dot(hidden, out_weight, preferred_element_type=jnp.float32)) * gains

def from_lower(faces_grid, axis_pos):
    extent = faces_grid.shape[axis_pos]
    zero_part = jnp.zeros_like(lax.slice_in_dim(faces_grid, 0, 1, axis=axis_pos))
    return jnp.concatenate([zero_part, lax.slice_in_dim(faces_grid, 0, extent - 1, axis=axis_pos)], axis=axis_pos)

def from_upper(faces_grid, axis_pos):
    extent = faces_grid.shape[axis_pos]
    zero_part = jnp.zeros_like(lax.slice_in_dim(faces_grid, 0, 1, axis=axis_pos))
    return jnp.concatenate([lax.slice_in_dim(faces_grid, 1, extent, axis=axis_pos), zero_part], axis=axis_pos)

def reference(fine_state, fine_nbrs, send_rows, ghost_counts, fine_parent, medium_state, medium_parent, coarse_state, coarse_nbrs, fine_edge_in, fine_edge_bias, fine_edge_out, fine_edge_gain, fine_node_in, fine_node_bias, fine_node_out, fine_node_gain, coarse_edge_in, coarse_edge_bias, coarse_edge_out, coarse_edge_gain, coarse_node_in, coarse_node_bias, coarse_node_out, coarse_node_gain):
    states = fine_state.reshape(DEVICES, NF_DEV, D)
    picked = jax.vmap(lambda rows_here, index_here: jnp.take(rows_here, index_here.reshape(-1), axis=0))(states, send_rows)
    picked = picked.reshape(DEVICES, 6, G, D)
    in_count = lax.broadcasted_iota(jnp.int32, (DEVICES, 6, G), 2) < ghost_counts[:, :, None]
    outgoing = jnp.where(in_count[:, :, :, None], picked, jnp.zeros_like(picked))
    grid = outgoing.reshape(GRID_X, GRID_Y, GRID_Z, 6, G, D)
    received = []
    for axis_pos in range(3):
        received.append(from_lower(grid[:, :, :, 2 * axis_pos + 1], axis_pos))
        received.append(from_upper(grid[:, :, :, 2 * axis_pos], axis_pos))
    ghosts = jnp.stack(received, axis=3).reshape(DEVICES, 6 * G, D)
    parents_all = fine_parent.reshape(DEVICES, NF_DEV)
    medium_parents_all = medium_parent.reshape(DEVICES, NM_DEV)

    def pool_device(inputs):
        own, parents, medium_here, medium_parents, coarse_here = inputs
        fine_member = parents[None, :] == lax.broadcasted_iota(jnp.int32, (NM_DEV, NF_DEV), 0)
        child_sum = jnp.dot(fine_member.astype(jnp.bfloat16), own, preferred_element_type=jnp.float32)
        child_count = lax.optimization_barrier(jnp.sum(fine_member.astype(jnp.float32), axis=1, keepdims=True))
        medium_pool = medium_here.astype(jnp.float32) + child_sum / child_count
        medium_member = (medium_parents[None, :] == lax.broadcasted_iota(jnp.int32, (NC_DEV, NM_DEV), 0)).astype(jnp.float32)
        coarse_sum = jnp.dot(medium_member, medium_pool, precision=lax.Precision.HIGHEST)
        coarse_pool = coarse_here.astype(jnp.float32) + coarse_sum / lax.optimization_barrier(jnp.sum(medium_member, axis=1, keepdims=True))
        return (medium_pool, coarse_pool.astype(jnp.bfloat16))
    medium_pools, coarse_pools = lax.map(pool_device, (states, parents_all, medium_state.reshape(DEVICES, NM_DEV, D), medium_parents_all, coarse_state.reshape(DEVICES, NC_DEV, D)))
    coarse_all = coarse_pools.reshape(NC, D)
    coarse_projected = jnp.dot(coarse_all, coarse_edge_in[:D], preferred_element_type=jnp.float32).astype(jnp.bfloat16)

    def main_device(inputs):
        own, ghost_rows, neighbours, parents, medium_pool, medium_parents, coarse_pool, coarse_links = inputs
        lookup = jnp.concatenate([own, ghost_rows, jnp.zeros((1, D), jnp.bfloat16)], axis=0)
        sender = jnp.dot(lookup, fine_edge_in[:D], preferred_element_type=jnp.float32).astype(jnp.bfloat16)
        receiver = jnp.dot(own, fine_edge_in[D:], preferred_element_type=jnp.float32)
        messages = edge_messages(jnp.take(sender, neighbours.reshape(-1), axis=0), receiver, fine_edge_bias, fine_edge_out, fine_edge_gain, K)
        live_slots = (neighbours < NF_DEV + 6 * G).astype(jnp.float32)
        incoming = lax.optimization_barrier(jnp.sum(messages.reshape(NF_DEV, K, D) * live_slots[:, :, None], axis=1)).astype(jnp.bfloat16)
        fine_new = own.astype(jnp.float32) + node_update(own, incoming, fine_node_in, fine_node_bias, fine_node_out, fine_node_gain)
        coarse_sender = jnp.take(coarse_projected, coarse_links.reshape(-1), axis=0)
        coarse_receiver = jnp.dot(coarse_pool, coarse_edge_in[D:], preferred_element_type=jnp.float32)
        coarse_msgs = edge_messages(coarse_sender, coarse_receiver, coarse_edge_bias, coarse_edge_out, coarse_edge_gain, KC)
        coarse_incoming = lax.optimization_barrier(jnp.sum(coarse_msgs.reshape(NC_DEV, KC, D), axis=1)).astype(jnp.bfloat16)
        coarse_delta = node_update(coarse_pool, coarse_incoming, coarse_node_in, coarse_node_bias, coarse_node_out, coarse_node_gain)
        coarse_new = (coarse_pool.astype(jnp.float32) + coarse_delta).astype(jnp.bfloat16)
        medium_delta = jnp.take(coarse_delta, medium_parents, axis=0)
        medium_new = (medium_pool + medium_delta).astype(jnp.bfloat16)
        fine_final = (fine_new + jnp.take(medium_delta, parents, axis=0)).astype(jnp.bfloat16)
        return (fine_final, medium_new, coarse_new)
    fine_outs, medium_outs, coarse_outs = lax.map(main_device, (states, ghosts, fine_nbrs.reshape(DEVICES, NF_DEV, K), parents_all, medium_pools, medium_parents_all, coarse_pools, coarse_nbrs.reshape(DEVICES, NC_DEV, KC)))
    return (fine_outs.reshape(NF, D), medium_outs.reshape(NM, D), coarse_outs.reshape(NC, D))
```

```python
import functools
import itertools

import jax
import jax.numpy as jnp
from jax import lax
from jax.experimental import pallas as pl
from jax.experimental.pallas import tpu as pltpu
from jax.sharding import Mesh
from jax.sharding import PartitionSpec as P

AXES = ("x", "zh", "c", "y", "z")
SIZES = (4, 2, 2, 4, 4)
EPS = 1e-05
F32 = jnp.float32
BF16 = jnp.bfloat16
D = 512
CHUNKS = 4
BLOCK = 128


def linear(place):
    number = 0
    for size, at in zip(SIZES, place):
        number = number * size + at
    return number


def permutation(move):
    pairs = []
    for place in itertools.product(*(range(size) for size in SIZES)):
        target = move(*place)
        if target is not None:
            pairs.append((linear(place), linear(target)))
    return pairs


def along_z(x, zh, c, y, z, step):
    at = (zh * 4 + z + step) % 8
    return (x, at // 4, c, y, at % 4)


def along_plane(x, zh, c, y, z, step, first):
    if (c == 0) == first:
        return ((x + step) % 4, zh, c, y, z)
    return (x, zh, c, (y + step) % 4, z)


SWAP = permutation(lambda x, zh, c, y, z: (x, zh, 1 - c, y, z))
RING = permutation(lambda x, zh, c, y, z: along_z(x, zh, c, y, z, 1 if c == 0 else -1))
RING_END = permutation(lambda x, zh, c, y, z: along_z(x, zh, c, y, z, -1) if c == 1 else None)
UP_FIRST = permutation(functools.partial(along_plane, step=1, first=True))
DOWN_FIRST = permutation(functools.partial(along_plane, step=-1, first=True))
UP_SECOND = permutation(functools.partial(along_plane, step=1, first=False))
DOWN_SECOND = permutation(functools.partial(along_plane, step=-1, first=False))


def dot(a, b):
    return lax.dot_general(a, b, (((1,), (0,)), ((), ())), preferred_element_type=F32)


def dot_t(a, b):
    return lax.dot_general(a, b, (((0,), (0,)), ((), ())), preferred_element_type=F32)


def normed(values):
    center = values - jnp.mean(values, axis=-1, keepdims=True)
    spread = jnp.mean(center * center, axis=-1, keepdims=True)
    return center * lax.rsqrt(spread + EPS)


def pool_kernel(
    fine, parent, medium, medium_parent, coarse, nbrs, weight,
    sender_out, pool_out, medium_out, slots_out, comp_out, member_out,
):
    member = (parent[...] == lax.broadcasted_iota(jnp.int32, (128, 1024), 0)).astype(F32)
    count = jnp.sum(member, axis=1, keepdims=True)
    member = member.astype(BF16)
    medium_pool = medium[...].astype(F32) + dot(member, fine[...]) / count
    medium_out[...] = medium_pool
    upper = (medium_parent[...] == lax.broadcasted_iota(jnp.int32, (16, 128), 0)).astype(F32)
    upper_count = jnp.sum(upper, axis=1, keepdims=True)
    total = jnp.dot(upper, medium_pool, precision=lax.Precision.HIGHEST, preferred_element_type=F32)
    pool = (coarse[...].astype(F32) + total / upper_count).astype(BF16)
    pool_out[...] = pool
    sender_out[...] = dot(pool, weight[...]).astype(BF16)
    upper = upper.astype(BF16)
    member_out[...] = jnp.concatenate([upper, upper], axis=0)
    comp = dot(upper, member).astype(BF16)
    comp_out[...] = jnp.concatenate([comp, comp], axis=0)
    here = {name: lax.axis_index(name) for name in AXES}
    row = nbrs[...] & 15
    owner = nbrs[...] >> 4
    z = owner & 3
    y = (owner >> 2) & 3
    c = (owner >> 4) & 1
    zh = (owner >> 5) & 1
    x = owner >> 6
    back = (here["zh"] * 4 + here["z"] - zh * 4 - z) & 7
    stream = (back > 3).astype(jnp.int32)
    at = jnp.where(stream == 0, back, 7 - back) * 32 + c * 16 + row
    step_x = (here["x"] - x) & 3
    step_y = (here["y"] - y) & 3
    order_x = jnp.where(step_x == 2, 3, jnp.where(step_x == 3, 2, step_x))
    order_y = jnp.where(step_y == 2, 3, jnp.where(step_y == 3, 2, step_y))
    at = at + jnp.where(stream == 0, order_x * 128 + order_y * 512, order_y * 128 + order_x * 512)
    slots_out[...] = at + jnp.where(stream == here["c"], 0, 2048)


def face_kernel(fine, rows, counts, weight, edge_out, sender_out, faces_out, centred_out):
    sender = dot(fine[...], weight[...]).astype(BF16)
    sender_out[...] = sender
    wide = edge_out[...].astype(F32)
    centred_out[...] = (wide - jnp.mean(wide, axis=1, keepdims=True)).astype(BF16)
    flat = jnp.concatenate([rows[0], jnp.zeros((2, 128), jnp.int32)], axis=0)
    columns = flat.T
    place = lax.broadcasted_iota(jnp.int32, (128, 1), 0)
    for face in range(6):
        wanted = jnp.where(place < counts[0, face], columns[:, face : face + 1], -1)
        picked = (wanted == lax.broadcasted_iota(jnp.int32, (128, 1024), 1)).astype(F32).astype(BF16)
        faces_out[face] = dot(picked, sender).astype(BF16)


def edge_kernel(
    sender, g0, g1, g2, g3, g4, g5, fine, nbrs, receive, bias, centred, gain,
    node_in, node_bias, node_out, node_gain,
    new_out,
    table, centred_v, node_in_v, node_out_v, sems,
):
    copies = [pltpu.make_async_copy(sender, table.at[pl.ds(0, 1024)], sems.at[0])]
    for k, ghost in enumerate((g0, g1, g2, g3, g4, g5)):
        copies.append(pltpu.make_async_copy(ghost.at[0], table.at[pl.ds(1024 + 128 * k, 128)], sems.at[1 + k]))
    copies.append(pltpu.make_async_copy(centred, centred_v, sems.at[7]))
    copies.append(pltpu.make_async_copy(node_in, node_in_v, sems.at[8]))
    copies.append(pltpu.make_async_copy(node_out, node_out_v, sems.at[9]))
    for copy in copies:
        copy.start()
    for copy in copies:
        copy.wait()
    rows = new_out.shape[0]

    def step(block, carry):
        span = pl.ds(pl.multiple_of(block * BLOCK, BLOCK), BLOCK)
        own = fine[span, :]
        near = nbrs[span, :]
        received = dot(own, receive[...]) + bias[...]
        total = jnp.zeros((BLOCK, D), F32)
        for k in range(6):
            wanted = near[:, k : k + 1]
            picked = (wanted == lax.broadcasted_iota(jnp.int32, (BLOCK, 1792), 1)).astype(F32).astype(BF16)
            found = dot(picked, table[...]).astype(BF16).astype(F32)
            hidden = jnp.maximum(found + received, 0.0).astype(BF16)
            out = dot(hidden, centred_v[...])
            spread = jnp.mean(out * out, axis=-1, keepdims=True)
            scale = lax.rsqrt(spread + EPS) * (wanted < 1792).astype(F32)
            total = total + out * scale
        incoming = (total * gain[...]).astype(BF16)
        both = jnp.concatenate([own, incoming], axis=1)
        hidden = jnp.maximum(dot(both, node_in_v[...]) + node_bias[...], 0.0).astype(BF16)
        new_out[span, :] = own.astype(F32) + normed(dot(hidden, node_out_v[...])) * node_gain[...]
        return carry

    lax.fori_loop(0, rows // BLOCK, step, 0)


def coarse_kernel(
    mine, other, slots, pool, medium, comp, member, n0, n1, n2, n3,
    edge_in, edge_bias, edge_out, edge_gain, node_in, node_bias, node_out, node_gain,
    fine_out, medium_out, coarse_out,
):
    pool_rows = pool[...]
    received = dot(pool_rows, edge_in[...]) + edge_bias[...]
    places = slots[...]
    column = jnp.concatenate([jnp.broadcast_to(places[:, k : k + 1], (16, 128)) for k in range(64)], axis=0)
    total = jnp.zeros((1024, D), F32)
    lane = lax.broadcasted_iota(jnp.int32, (1024, 128), 1)
    for piece in range(8):
        source = mine if piece < 4 else other
        picked = jnp.concatenate(
            [(column == lane + (piece * 512 + t * 128)).astype(F32).astype(BF16) for t in range(4)], axis=1
        )
        total = total + dot(picked, source[(piece % 4) * 512 : (piece % 4 + 1) * 512, :])
    hidden = jnp.maximum(total.reshape(64, 16, D) + received[None], 0.0).astype(BF16).reshape(1024, D)
    message = normed(dot(hidden, edge_out[...])) * edge_gain[...]
    incoming = jnp.sum(message.reshape(64, 16, D), axis=0).astype(BF16)
    both = jnp.concatenate([pool_rows, incoming], axis=1)
    hidden = jnp.maximum(dot(both, node_in[...]) + node_bias[...], 0.0).astype(BF16)
    delta = normed(dot(hidden, node_out[...])) * node_gain[...]
    coarse_out[...] = (pool_rows.astype(F32) + delta).astype(BF16)
    high = delta.astype(BF16)
    low = (delta - high.astype(F32)).astype(BF16)
    parts = jnp.concatenate([high, low], axis=0)
    medium_out[...] = (medium[...] + dot_t(member[...], parts)).astype(BF16)
    spread = dot_t(comp[...], parts)
    for k, new in enumerate((n0, n1, n2, n3)):
        fine_out[k * 256 : (k + 1) * 256, :] = (new[...] + spread[k * 256 : (k + 1) * 256]).astype(BF16)


def joined(*parts):
    return jnp.concatenate(parts, axis=0)


def sent(rows, pairs):
    return lax.ppermute(rows, AXES, pairs)


def local(
    fine_state, fine_nbrs, send_rows, ghost_counts, fine_parent, medium_state, medium_parent, coarse_state,
    coarse_nbrs, fine_edge_in, fine_edge_bias, fine_edge_out, fine_edge_gain, fine_node_in, fine_node_bias,
    fine_node_out, fine_node_gain, coarse_edge_in, coarse_edge_bias, coarse_edge_out, coarse_edge_gain,
    coarse_node_in, coarse_node_bias, coarse_node_out, coarse_node_gain,
):
    vmem, smem, anywhere = pltpu.VMEM, pltpu.SMEM, pl.ANY
    row = lambda vector: vector.reshape(1, -1)
    lower = pl.BlockSpec((D, D), lambda i: (0, 0), memory_space=vmem)

    sender, pool, medium_pool, slots, comp, member = pl.pallas_call(
        pool_kernel,
        grid=(1,),
        out_shape=[
            jax.ShapeDtypeStruct((16, D), BF16),
            jax.ShapeDtypeStruct((16, D), BF16),
            jax.ShapeDtypeStruct((128, D), F32),
            jax.ShapeDtypeStruct((16, 64), jnp.int32),
            jax.ShapeDtypeStruct((32, 1024), BF16),
            jax.ShapeDtypeStruct((32, 128), BF16),
        ],
        in_specs=[pl.BlockSpec(memory_space=vmem)] * 6 + [lower],
        out_specs=[pl.BlockSpec(memory_space=vmem)] * 6,
        compiler_params=pltpu.CompilerParams(vmem_limit_bytes=32 << 20),
    )(fine_state, row(fine_parent), medium_state, row(medium_parent), coarse_state, coarse_nbrs, coarse_edge_in)

    fine_sender, faces, centred = pl.pallas_call(
        face_kernel,
        grid=(1,),
        out_shape=[
            jax.ShapeDtypeStruct((1024, D), BF16),
            jax.ShapeDtypeStruct((6, 128, D), BF16),
            jax.ShapeDtypeStruct((D, D), BF16),
        ],
        in_specs=[
            pl.BlockSpec(memory_space=vmem),
            pl.BlockSpec(memory_space=vmem),
            pl.BlockSpec(memory_space=smem),
            lower,
            pl.BlockSpec(memory_space=vmem),
        ],
        out_specs=[pl.BlockSpec(memory_space=vmem)] * 3,
        compiler_params=pltpu.CompilerParams(vmem_limit_bytes=32 << 20),
    )(fine_state, send_rows, ghost_counts, fine_edge_in, fine_edge_out)

    ghosts = []
    for face, axes in ((0, ("x", "zh", "c")), (2, "y"), (4, "z")):
        count = lax.axis_size(axes)
        forward = [(k, k + 1) for k in range(count - 1)]
        backward = [(k + 1, k) for k in range(count - 1)]
        ghosts.append(lax.ppermute(faces[face + 1 : face + 2], axes, forward))
        ghosts.append(lax.ppermute(faces[face : face + 1], axes, backward))

    core = lax.axis_index("c")
    beside = sent(sender, SWAP)
    chip = jnp.where(core == 0, joined(sender, beside), joined(beside, sender))
    ring = [chip]
    for _ in range(3):
        ring.append(sent(ring[-1], RING))
    last = sent(ring[-1], RING_END)
    column = jnp.where(core == 0, joined(*ring), joined(*ring[1:], last))
    up, down = sent(column, UP_FIRST), sent(column, DOWN_FIRST)
    line = joined(column, up, down, sent(up[:64], UP_FIRST), sent(down[64:], DOWN_FIRST))
    up, down = sent(line, UP_SECOND), sent(line, DOWN_SECOND)
    mine = joined(line, up, down, sent(up[:256], UP_SECOND), sent(down[256:], DOWN_SECOND))
    other = sent(mine, SWAP)

    news = []
    span = 1024 // CHUNKS
    for chunk in range(CHUNKS):
        part = pl.BlockSpec((span, D), lambda i, chunk=chunk: (chunk, 0), memory_space=vmem)
        near = pl.BlockSpec((span, 6), lambda i, chunk=chunk: (chunk, 0), memory_space=vmem)
        whole = pl.BlockSpec(memory_space=vmem)
        left = pl.BlockSpec(memory_space=anywhere)
        news.append(
            pl.pallas_call(
                edge_kernel,
                grid=(1,),
                out_shape=jax.ShapeDtypeStruct((span, D), F32),
                in_specs=[left] * 7
                + [part, near, pl.BlockSpec((D, D), lambda i: (1, 0), memory_space=vmem), whole, left, whole, left, whole, left, whole],
                out_specs=whole,
                scratch_shapes=[
                    pltpu.VMEM((1792, D), BF16),
                    pltpu.VMEM((D, D), BF16),
                    pltpu.VMEM((2 * D, D), BF16),
                    pltpu.VMEM((D, D), BF16),
                    pltpu.SemaphoreType.DMA((10,)),
                ],
                compiler_params=pltpu.CompilerParams(vmem_limit_bytes=32 << 20),
                cost_estimate=pl.CostEstimate(flops=3_500_000_000, bytes_accessed=5_000_000, transcendentals=0),
            )(
                fine_sender, *ghosts, fine_state, fine_nbrs, fine_edge_in, row(fine_edge_bias), centred,
                row(fine_edge_gain), fine_node_in, row(fine_node_bias), fine_node_out, row(fine_node_gain),
            )
        )

    whole = pl.BlockSpec(memory_space=vmem)
    fine_out, medium_out, coarse_out = pl.pallas_call(
        coarse_kernel,
        grid=(1,),
        out_shape=[
            jax.ShapeDtypeStruct((1024, D), BF16),
            jax.ShapeDtypeStruct((128, D), BF16),
            jax.ShapeDtypeStruct((16, D), BF16),
        ],
        in_specs=[whole] * 11 + [pl.BlockSpec((D, D), lambda i: (1, 0), memory_space=vmem)] + [whole] * 7,
        out_specs=[whole] * 3,
        compiler_params=pltpu.CompilerParams(vmem_limit_bytes=48 << 20),
    )(
        mine, other, slots, pool, medium_pool, comp, member, *news, coarse_edge_in, row(coarse_edge_bias),
        coarse_edge_out, row(coarse_edge_gain), coarse_node_in, row(coarse_node_bias), coarse_node_out,
        row(coarse_node_gain),
    )
    return fine_out, medium_out, coarse_out


def solution(mesh):
    torus = Mesh(mesh.devices.reshape(SIZES), AXES)
    rows = P(AXES, None)
    placed = (rows, rows, P(AXES, None, None), rows, P(AXES), rows, P(AXES), rows, rows) + (P(),) * 16
    return jax.shard_map(local, mesh=torus, in_specs=placed, out_specs=(rows, rows, rows), check_vma=False)
```

```python
import functools
import itertools

import jax
import jax.numpy as jnp
from jax import lax
from jax.experimental import pallas as pl
from jax.experimental.pallas import tpu as pltpu
from jax.sharding import Mesh
from jax.sharding import PartitionSpec as P

AXES = ("x", "zh", "c", "y", "z")
SIZES = (4, 2, 2, 4, 4)
EPS = 1e-05
F32 = jnp.float32
BF16 = jnp.bfloat16
D = 512
BLOCK = 128
SHARES = (2, 2, 2, 2)


def linear(place):
    number = 0
    for size, at in zip(SIZES, place):
        number = number * size + at
    return number


def permutation(move):
    pairs = []
    for place in itertools.product(*(range(size) for size in SIZES)):
        target = move(*place)
        if target is not None:
            pairs.append((linear(place), linear(target)))
    return pairs


def along_z(x, zh, c, y, z, step):
    at = (zh * 4 + z + step) % 8
    return (x, at // 4, c, y, at % 4)


def along_plane(x, zh, c, y, z, step, first):
    if (c == 0) == first:
        return ((x + step) % 4, zh, c, y, z)
    return (x, zh, c, (y + step) % 4, z)


SWAP = permutation(lambda x, zh, c, y, z: (x, zh, 1 - c, y, z))
RING = permutation(lambda x, zh, c, y, z: along_z(x, zh, c, y, z, 1 if c == 0 else -1))
RING_END = permutation(lambda x, zh, c, y, z: along_z(x, zh, c, y, z, -1) if c == 1 else None)
UP_FIRST = permutation(functools.partial(along_plane, step=1, first=True))
DOWN_FIRST = permutation(functools.partial(along_plane, step=-1, first=True))
UP_SECOND = permutation(functools.partial(along_plane, step=1, first=False))
DOWN_SECOND = permutation(functools.partial(along_plane, step=-1, first=False))


def dot(a, b):
    return lax.dot_general(a, b, (((1,), (0,)), ((), ())), preferred_element_type=F32)


def dot_t(a, b):
    return lax.dot_general(a, b, (((0,), (0,)), ((), ())), preferred_element_type=F32)


def normed(values):
    center = values - jnp.mean(values, axis=-1, keepdims=True)
    spread = jnp.mean(center * center, axis=-1, keepdims=True)
    return center * lax.rsqrt(spread + EPS)


def pool_kernel(
    fine_h, parent_h, medium_h, medium_parent_h, coarse_h, nbrs_h, weight_h,
    sender_out, pool_out, medium_out, slots_out, comp_out, member_out,
    fine, parent, medium, medium_parent, coarse, nbrs, weight, sems,
):
    pairs = (
        (parent_h, parent), (fine_h, fine), (medium_h, medium), (medium_parent_h, medium_parent),
        (coarse_h, coarse), (weight_h.at[pl.ds(0, D)], weight), (nbrs_h, nbrs),
    )
    copies = [pltpu.make_async_copy(source, target, sems.at[k]) for k, (source, target) in enumerate(pairs)]
    for copy in copies:
        copy.start()
    for copy in copies:
        copy.wait()
    member = (parent[...] == lax.broadcasted_iota(jnp.int32, (128, 1024), 0)).astype(F32)
    count = jnp.sum(member, axis=1, keepdims=True)
    member = member.astype(BF16)
    medium_pool = medium[...].astype(F32) + dot(member, fine[...]) / count
    medium_out[...] = medium_pool
    upper = (medium_parent[...] == lax.broadcasted_iota(jnp.int32, (16, 128), 0)).astype(F32)
    upper_count = jnp.sum(upper, axis=1, keepdims=True)
    total = jnp.dot(upper, medium_pool, precision=lax.Precision.HIGHEST, preferred_element_type=F32)
    pool = (coarse[...].astype(F32) + total / upper_count).astype(BF16)
    pool_out[...] = pool
    sender_out[...] = dot(pool, weight[...]).astype(BF16)
    upper = upper.astype(BF16)
    member_out[...] = jnp.concatenate([upper, upper], axis=0)
    comp = dot(upper, member).astype(BF16)
    comp_out[...] = jnp.concatenate([comp, comp], axis=0)
    here = {name: lax.axis_index(name) for name in AXES}
    row = nbrs[...] & 15
    owner = nbrs[...] >> 4
    z = owner & 3
    y = (owner >> 2) & 3
    c = (owner >> 4) & 1
    zh = (owner >> 5) & 1
    x = owner >> 6
    back = (here["zh"] * 4 + here["z"] - zh * 4 - z) & 7
    stream = (back > 3).astype(jnp.int32)
    at = jnp.where(stream == 0, back, 7 - back) * 32 + c * 16 + row
    step_x = (here["x"] - x) & 3
    step_y = (here["y"] - y) & 3
    order_x = jnp.where(step_x == 2, 3, jnp.where(step_x == 3, 2, step_x))
    order_y = jnp.where(step_y == 2, 3, jnp.where(step_y == 3, 2, step_y))
    at = at + jnp.where(stream == 0, order_x * 128 + order_y * 512, order_y * 128 + order_x * 512)
    slots_out[...] = at + jnp.where(stream == here["c"], 0, 2048)


def face_kernel(
    after, fine_h, rows_h, counts, weight_h, edge_out_h,
    sender_out, centred_out, f0, f1, f2, f3, f4, f5,
    fine, rows, weight, edge_out, sems,
):
    pairs = ((rows_h, rows), (fine_h, fine), (weight_h.at[pl.ds(0, D)], weight), (edge_out_h, edge_out))
    copies = [pltpu.make_async_copy(source, target, sems.at[k]) for k, (source, target) in enumerate(pairs)]
    for copy in copies:
        copy.start()
    for copy in copies:
        copy.wait()
    sender = dot(fine[...], weight[...]).astype(BF16)
    sender_out[...] = sender
    wide = edge_out[...].astype(F32)
    centred_out[...] = (wide - jnp.mean(wide, axis=1, keepdims=True)).astype(BF16)
    flat = jnp.concatenate(
        [rows[:, 128 * face : 128 * (face + 1)] for face in range(6)] + [jnp.zeros((2, 128), jnp.int32)], axis=0
    )
    columns = flat.T
    place = lax.broadcasted_iota(jnp.int32, (128, 1), 0)
    for face, face_out in enumerate((f0, f1, f2, f3, f4, f5)):
        wanted = jnp.where(place < counts[0, face], columns[:, face : face + 1], -1)
        picked = (wanted == lax.broadcasted_iota(jnp.int32, (128, 1024), 1)).astype(F32).astype(BF16)
        face_out[0] = dot(picked, sender).astype(BF16)


def table_kernel(sender, g0, g1, g2, g3, g4, g5, nbrs, table_out, near_out, sems):
    copies = [pltpu.make_async_copy(sender, table_out.at[pl.ds(0, 1024)], sems.at[0])]
    for k, ghost in enumerate((g0, g1, g2, g3, g4, g5)):
        copies.append(
            pltpu.make_async_copy(ghost.at[0], table_out.at[pl.ds(1024 + 128 * k, 128)], sems.at[1 + k])
        )
    for copy in copies:
        copy.start()
    padded = jnp.concatenate([nbrs[...], jnp.zeros((2, 1024), jnp.int32)], axis=0)
    for block in range(8):
        near_out[block * 128 : (block + 1) * 128, :] = padded[:, block * 128 : (block + 1) * 128].T
    for copy in copies:
        copy.wait()


def edge_kernel(
    table, fine, nbrs, receive, bias, centred, gain, node_in, node_bias, node_out, node_gain,
    new_out,
    picked, hidden,
    *, first,
):
    blocks = new_out.shape[0] // BLOCK

    def step(block, carry):
        here = pl.ds(pl.multiple_of(block * BLOCK, BLOCK), BLOCK)
        span = pl.ds(pl.multiple_of((first + block) * BLOCK, BLOCK), BLOCK)
        own = fine[span, :]
        near = nbrs[span, :]
        received = dot(own, receive[...]) + bias[...]
        for k in range(6):
            wanted = near[:, k : k + 1]
            match = wanted == lax.broadcasted_iota(jnp.int32, (BLOCK, 1792), 1)
            picked[k * BLOCK : (k + 1) * BLOCK, :] = match.astype(F32).astype(BF16)
        found = dot(picked[...], table[...]).astype(BF16).astype(F32)
        hidden[...] = jnp.maximum(found + jnp.concatenate([received] * 6, axis=0), 0.0).astype(BF16)
        out = dot(hidden[...], centred[...])
        out = out * lax.rsqrt(jnp.mean(out * out, axis=-1, keepdims=True) + EPS)
        total = jnp.zeros((BLOCK, D), F32)
        for k in range(6):
            total = total + out[k * BLOCK : (k + 1) * BLOCK] * (near[:, k : k + 1] < 1792).astype(F32)
        incoming = (total * gain[...]).astype(BF16)
        both = jnp.concatenate([own, incoming], axis=1)
        node = jnp.maximum(dot(both, node_in[...]) + node_bias[...], 0.0).astype(BF16)
        new_out[here, :] = own.astype(F32) + normed(dot(node, node_out[...])) * node_gain[...]
        return carry

    lax.fori_loop(0, blocks, step, 0)


def columns_of(slots):
    places = slots[...]
    return jnp.concatenate([jnp.broadcast_to(places[:, k : k + 1], (16, 128)) for k in range(64)], axis=0)


def found_in(column, sources):
    lane = lax.broadcasted_iota(jnp.int32, (1024, 128), 1)
    total = jnp.zeros((1024, D), F32)
    for start, source in sources:
        picked = [
            (column == lane + (start + t * 128)).astype(F32).astype(BF16) for t in range(source.shape[0] // 128)
        ]
        total = total + dot(jnp.concatenate(picked, axis=1), source[...])
    return total


def gather_kernel(slots, m0, m1, m2, m3, m4, found_out):
    sources = ((0, m0), (512, m1), (1024, m2), (1536, m3), (1792, m4))
    found_out[...] = found_in(columns_of(slots), sources).astype(BF16)


def coarse_kernel(
    found, o0, o1, o2, o3, o4, slots, pool, medium, comp, member, *rest,
):
    *news, edge_in, edge_bias, edge_out, edge_gain, node_in, node_bias, node_out, node_gain, fine_out, medium_out, coarse_out = rest
    pool_rows = pool[...]
    received = dot(pool_rows, edge_in[...]) + edge_bias[...]
    sources = ((2048, o0), (2560, o1), (3072, o2), (3584, o3), (3840, o4))
    total = found[...].astype(F32) + found_in(columns_of(slots), sources)
    hidden = jnp.maximum(total.reshape(64, 16, D) + received[None], 0.0).astype(BF16).reshape(1024, D)
    message = normed(dot(hidden, edge_out[...])) * edge_gain[...]
    incoming = jnp.sum(message.reshape(64, 16, D), axis=0).astype(BF16)
    both = jnp.concatenate([pool_rows, incoming], axis=1)
    hidden = jnp.maximum(dot(both, node_in[...]) + node_bias[...], 0.0).astype(BF16)
    delta = normed(dot(hidden, node_out[...])) * node_gain[...]
    coarse_out[...] = (pool_rows.astype(F32) + delta).astype(BF16)
    high = delta.astype(BF16)
    low = (delta - high.astype(F32)).astype(BF16)
    parts = jnp.concatenate([high, low], axis=0)
    medium_out[...] = (medium[...] + dot_t(member[...], parts)).astype(BF16)
    spread = dot_t(comp[...], parts)
    first = 0
    for new in news:
        last = first + new.shape[0]
        fine_out[first:last, :] = (new[...] + spread[first:last]).astype(BF16)
        first = last


def joined(*parts):
    return jnp.concatenate(parts, axis=0)


def sent(rows, pairs):
    return lax.ppermute(rows, AXES, pairs)


def local(
    fine_state, fine_nbrs, send_rows, ghost_counts, fine_parent, medium_state, medium_parent, coarse_state,
    coarse_nbrs, fine_edge_in, fine_edge_bias, fine_edge_out, fine_edge_gain, fine_node_in, fine_node_bias,
    fine_node_out, fine_node_gain, coarse_edge_in, coarse_edge_bias, coarse_edge_out, coarse_edge_gain,
    coarse_node_in, coarse_node_bias, coarse_node_out, coarse_node_gain,
):
    row = lambda vector: vector.reshape(1, -1)
    shaped = jax.ShapeDtypeStruct
    held = pl.BlockSpec(memory_space=pltpu.VMEM)
    far = pl.BlockSpec(memory_space=pltpu.HBM)
    scalars = pl.BlockSpec(memory_space=pltpu.SMEM)
    upper = pl.BlockSpec((D, D), lambda i: (1, 0), memory_space=pltpu.VMEM)
    tied = lax.optimization_barrier
    distant = functools.partial(pltpu.with_memory_space_constraint, memory_space=pltpu.HBM)

    def kernel(body, outs, specs, args, scratch=(), limit=32, cost=None):
        return pl.pallas_call(
            body,
            grid=(1,),
            out_shape=outs,
            in_specs=specs,
            out_specs=[held] * len(outs),
            scratch_shapes=list(scratch),
            compiler_params=pltpu.CompilerParams(vmem_limit_bytes=limit << 20),
            cost_estimate=cost,
        )(*args)

    sender, pool, medium_pool, slots, comp, member = kernel(
        pool_kernel,
        [
            shaped((16, D), BF16),
            shaped((16, D), BF16),
            shaped((128, D), F32),
            shaped((16, 64), jnp.int32),
            shaped((32, 1024), BF16),
            shaped((32, 128), BF16),
        ],
        [far] * 7,
        [
            distant(value)
            for value in (
                fine_state, row(fine_parent), medium_state, row(medium_parent), coarse_state, coarse_nbrs,
                coarse_edge_in,
            )
        ],
        [
            pltpu.VMEM((1024, D), BF16),
            pltpu.VMEM((1, 1024), jnp.int32),
            pltpu.VMEM((128, D), BF16),
            pltpu.VMEM((1, 128), jnp.int32),
            pltpu.VMEM((16, D), BF16),
            pltpu.VMEM((16, 64), jnp.int32),
            pltpu.VMEM((D, D), BF16),
            pltpu.SemaphoreType.DMA((7,)),
        ],
    )
    fine_sender, centred, *faces = kernel(
        face_kernel,
        [shaped((1024, D), BF16), shaped((D, D), BF16)] + [shaped((1, 128, D), BF16)] * 6,
        [pl.BlockSpec(memory_space=pl.ANY), far, far, scalars, far, far],
        (
            member, distant(fine_state), distant(send_rows.reshape(1, 768)), ghost_counts, distant(fine_edge_in),
            distant(fine_edge_out),
        ),
        [
            pltpu.VMEM((1024, D), BF16),
            pltpu.VMEM((1, 768), jnp.int32),
            pltpu.VMEM((D, D), BF16),
            pltpu.VMEM((D, D), BF16),
            pltpu.SemaphoreType.DMA((4,)),
        ],
    )

    def faced(block, face):
        axes = (("x", "zh", "c"), "y", "z")[face // 2]
        count = lax.axis_size(axes)
        pairs = [(k, k + 1) for k in range(count - 1)]
        return lax.ppermute(block, axes, [(b, a) for a, b in pairs] if face % 2 == 0 else pairs)

    core = lax.axis_index("c")
    beside = sent(sender, SWAP)
    chip = jnp.where(core == 0, joined(sender, beside), joined(beside, sender))
    ring = [chip]
    ghosts = {}
    for hop, group in enumerate(((1,), (0,), (3, 2), (5, 4))):
        carried = ring[-1]
        blocks = [faces[face] for face in group]
        carried, *blocks = tied((carried, *blocks))
        ring.append(sent(carried, RING if hop < 3 else RING_END))
        for face, block in zip(group, blocks):
            ghosts[face] = faced(block, face)
    last = ring.pop()
    column = jnp.where(core == 0, joined(*ring), joined(*ring[1:], last))
    near_faces = [ghosts[face] for face in (1, 0, 3, 2, 5, 4)]
    fine_sender, column = tied((fine_sender, column))
    table, near = kernel(
        table_kernel,
        [shaped((1792, D), BF16), shaped((1024, 8), jnp.int32)],
        [pl.BlockSpec(memory_space=pl.ANY)] * 7 + [held],
        (fine_sender, *near_faces, fine_nbrs.T),
        [pltpu.SemaphoreType.DMA((7,))],
    )
    news = []

    def edges(blocks):
        first = sum(new.shape[0] for new in news) // BLOCK
        news.extend(
            kernel(
                functools.partial(edge_kernel, first=first),
                [shaped((blocks * BLOCK, D), F32)],
                [held] * 3 + [upper] + [held] * 7,
                (
                    table, fine_state, near, fine_edge_in, row(fine_edge_bias), centred, row(fine_edge_gain),
                    fine_node_in, row(fine_node_bias), fine_node_out, row(fine_node_gain),
                ),
                [pltpu.VMEM((6 * BLOCK, 1792), BF16), pltpu.VMEM((6 * BLOCK, D), BF16)],
                cost=pl.CostEstimate(
                    flops=blocks * 1_700_000_000, bytes_accessed=blocks * 3_000_000, transcendentals=0
                ),
            )
        )

    up, down = sent(column, UP_FIRST), sent(column, DOWN_FIRST)
    edges(SHARES[0])
    up, down, news[-1] = tied((up, down, news[-1]))
    table, up = tied((table, up))
    rest = [sent(up[:64], UP_FIRST), sent(down[64:], DOWN_FIRST)]
    edges(SHARES[1])
    *rest, news[-1] = tied((*rest, news[-1]))
    line = joined(column, up, down, *rest)
    table, line = tied((table, line))
    up, down = sent(line, UP_SECOND), sent(line, DOWN_SECOND)
    others = [sent(line, SWAP)]
    edges(SHARES[2])
    up, down, news[-1] = tied((up, down, news[-1]))
    table, up = tied((table, up))
    rest = [sent(up[:256], UP_SECOND), sent(down[256:], DOWN_SECOND)]
    others += [sent(up, SWAP), sent(down, SWAP)]
    edges(SHARES[3])
    *rest, news[-1] = tied((*rest, news[-1]))
    others += [sent(part, SWAP) for part in rest]
    (found,) = kernel(
        gather_kernel, [shaped((1024, D), BF16)], [held] * 6, (slots, line, up, down, *rest), limit=40,
        cost=pl.CostEstimate(flops=2_000_000_000, bytes_accessed=4_000_000, transcendentals=0),
    )
    fine_out, medium_out, coarse_out = kernel(
        coarse_kernel,
        [shaped((1024, D), BF16), shaped((128, D), BF16), shaped((16, D), BF16)],
        [held] * (11 + len(news)) + [upper] + [held] * 7,
        (
            found, *others, slots, pool, medium_pool, comp, member, *news, coarse_edge_in, row(coarse_edge_bias),
            coarse_edge_out, row(coarse_edge_gain), coarse_node_in, row(coarse_node_bias), coarse_node_out,
            row(coarse_node_gain),
        ),
        limit=48,
    )
    return fine_out, medium_out, coarse_out


def solution(mesh):
    torus = Mesh(mesh.devices.reshape(SIZES), AXES)
    rows = P(AXES, None)
    placed = (rows, rows, P(AXES, None, None), rows, P(AXES), rows, P(AXES), rows, rows) + (P(),) * 16
    return jax.shard_map(local, mesh=torus, in_specs=placed, out_specs=(rows, rows, rows), check_vma=False)
```

```python
import functools
import itertools

import jax
import jax.numpy as jnp
from jax import lax
from jax.experimental import pallas as pl
from jax.experimental.pallas import tpu as pltpu
from jax.sharding import Mesh
from jax.sharding import PartitionSpec as P

AXES = ("x", "zh", "c", "y", "z")
SIZES = (4, 2, 2, 4, 4)
EPS = 1e-05
F32 = jnp.float32
BF16 = jnp.bfloat16
D = 512
BLOCK = 128
SHARES = (2, 2, 2, 2)


def linear(place):
    number = 0
    for size, at in zip(SIZES, place):
        number = number * size + at
    return number


def permutation(move):
    pairs = []
    for place in itertools.product(*(range(size) for size in SIZES)):
        target = move(*place)
        if target is not None:
            pairs.append((linear(place), linear(target)))
    return pairs


def along_z(x, zh, c, y, z, step):
    at = (zh * 4 + z + step) % 8
    return (x, at // 4, c, y, at % 4)


def along_plane(x, zh, c, y, z, step, first):
    if (c == 0) == first:
        return ((x + step) % 4, zh, c, y, z)
    return (x, zh, c, (y + step) % 4, z)


SWAP = permutation(lambda x, zh, c, y, z: (x, zh, 1 - c, y, z))
UP_Z = permutation(functools.partial(along_z, step=1))
DOWN_Z = permutation(functools.partial(along_z, step=-1))
UP_FIRST = permutation(functools.partial(along_plane, step=1, first=True))
DOWN_FIRST = permutation(functools.partial(along_plane, step=-1, first=True))
UP_SECOND = permutation(functools.partial(along_plane, step=1, first=False))
DOWN_SECOND = permutation(functools.partial(along_plane, step=-1, first=False))


def dot(a, b):
    return lax.dot_general(a, b, (((1,), (0,)), ((), ())), preferred_element_type=F32)


def dot_t(a, b):
    return lax.dot_general(a, b, (((0,), (0,)), ((), ())), preferred_element_type=F32)


def normed(values):
    center = values - jnp.mean(values, axis=-1, keepdims=True)
    spread = jnp.mean(center * center, axis=-1, keepdims=True)
    return center * lax.rsqrt(spread + EPS)


def pool_kernel(
    fine_h, parent_h, medium_h, medium_parent_h, coarse_h, nbrs_h, weight_h,
    sender_out, pool_out, medium_out, slots_out, comp_out, member_out,
    fine, parent, medium, medium_parent, coarse, nbrs, weight, sems,
):
    pairs = (
        (parent_h, parent), (fine_h, fine), (medium_h, medium), (medium_parent_h, medium_parent),
        (coarse_h, coarse), (weight_h.at[pl.ds(0, D)], weight), (nbrs_h, nbrs),
    )
    copies = [pltpu.make_async_copy(source, target, sems.at[k]) for k, (source, target) in enumerate(pairs)]
    for copy in copies:
        copy.start()
    for copy in copies:
        copy.wait()
    member = (parent[...] == lax.broadcasted_iota(jnp.int32, (128, 1024), 0)).astype(F32)
    count = jnp.sum(member, axis=1, keepdims=True)
    member = member.astype(BF16)
    medium_pool = medium[...].astype(F32) + dot(member, fine[...]) / count
    medium_out[...] = medium_pool
    upper = (medium_parent[...] == lax.broadcasted_iota(jnp.int32, (16, 128), 0)).astype(F32)
    upper_count = jnp.sum(upper, axis=1, keepdims=True)
    total = jnp.dot(upper, medium_pool, precision=lax.Precision.HIGHEST, preferred_element_type=F32)
    pool = (coarse[...].astype(F32) + total / upper_count).astype(BF16)
    pool_out[...] = pool
    sender_out[...] = dot(pool, weight[...]).astype(BF16)
    upper = upper.astype(BF16)
    member_out[...] = jnp.concatenate([upper, upper], axis=0)
    comp = dot(upper, member).astype(BF16)
    comp_out[...] = jnp.concatenate([comp, comp], axis=0)
    here = {name: lax.axis_index(name) for name in AXES}
    row = nbrs[...] & 15
    owner = nbrs[...] >> 4
    z = owner & 3
    y = (owner >> 2) & 3
    c = (owner >> 4) & 1
    zh = (owner >> 5) & 1
    x = owner >> 6
    back = (here["zh"] * 4 + here["z"] - zh * 4 - z) & 7
    stream = c
    at = jnp.where(back <= 4, back, 12 - back) * 16 + row
    step_x = (here["x"] - x) & 3
    step_y = (here["y"] - y) & 3
    order_x = jnp.where(step_x == 2, 3, jnp.where(step_x == 3, 2, step_x))
    order_y = jnp.where(step_y == 2, 3, jnp.where(step_y == 3, 2, step_y))
    at = at + jnp.where(stream == 0, order_x * 128 + order_y * 512, order_y * 128 + order_x * 512)
    slots_out[...] = at + jnp.where(stream == here["c"], 0, 2048)


def face_kernel(
    after, fine_h, rows_h, counts, weight_h, edge_out_h,
    sender_out, centred_out, f0, f1, f2, f3, f4, f5,
    fine, rows, weight, edge_out, sems,
):
    pairs = ((rows_h, rows), (fine_h, fine), (weight_h.at[pl.ds(0, D)], weight), (edge_out_h, edge_out))
    copies = [pltpu.make_async_copy(source, target, sems.at[k]) for k, (source, target) in enumerate(pairs)]
    for copy in copies:
        copy.start()
    for copy in copies:
        copy.wait()
    sender = dot(fine[...], weight[...]).astype(BF16)
    sender_out[...] = sender
    wide = edge_out[...].astype(F32)
    centred_out[...] = (wide - jnp.mean(wide, axis=1, keepdims=True)).astype(BF16)
    flat = jnp.concatenate(
        [rows[:, 128 * face : 128 * (face + 1)] for face in range(6)] + [jnp.zeros((2, 128), jnp.int32)], axis=0
    )
    columns = flat.T
    place = lax.broadcasted_iota(jnp.int32, (128, 1), 0)
    for face, face_out in enumerate((f0, f1, f2, f3, f4, f5)):
        wanted = jnp.where(place < counts[0, face], columns[:, face : face + 1], -1)
        picked = (wanted == lax.broadcasted_iota(jnp.int32, (128, 1024), 1)).astype(F32).astype(BF16)
        face_out[0] = dot(picked, sender).astype(BF16)


def table_kernel(sender, g0, g1, g2, g3, g4, g5, nbrs, table_out, near_out, sems):
    copies = [pltpu.make_async_copy(sender, table_out.at[pl.ds(0, 1024)], sems.at[0])]
    for k, ghost in enumerate((g0, g1, g2, g3, g4, g5)):
        copies.append(
            pltpu.make_async_copy(ghost.at[0], table_out.at[pl.ds(1024 + 128 * k, 128)], sems.at[1 + k])
        )
    for copy in copies:
        copy.start()
    padded = jnp.concatenate([nbrs[...], jnp.zeros((2, 1024), jnp.int32)], axis=0)
    for block in range(8):
        near_out[block * 128 : (block + 1) * 128, :] = padded[:, block * 128 : (block + 1) * 128].T
    for copy in copies:
        copy.wait()


def edge_kernel(
    table, fine, nbrs, receive, bias, centred, gain, node_in, node_bias, node_out, node_gain,
    new_out,
    picked, hidden,
    *, first,
):
    blocks = new_out.shape[0] // BLOCK

    def step(block, carry):
        here = pl.ds(pl.multiple_of(block * BLOCK, BLOCK), BLOCK)
        span = pl.ds(pl.multiple_of((first + block) * BLOCK, BLOCK), BLOCK)
        own = fine[span, :]
        near = nbrs[span, :]
        received = dot(own, receive[...]) + bias[...]
        for k in range(6):
            wanted = near[:, k : k + 1]
            match = wanted == lax.broadcasted_iota(jnp.int32, (BLOCK, 1792), 1)
            picked[k * BLOCK : (k + 1) * BLOCK, :] = match.astype(F32).astype(BF16)
        found = dot(picked[...], table[...]).astype(BF16).astype(F32)
        hidden[...] = jnp.maximum(found + jnp.concatenate([received] * 6, axis=0), 0.0).astype(BF16)
        out = dot(hidden[...], centred[...])
        out = out * lax.rsqrt(jnp.mean(out * out, axis=-1, keepdims=True) + EPS)
        total = jnp.zeros((BLOCK, D), F32)
        for k in range(6):
            total = total + out[k * BLOCK : (k + 1) * BLOCK] * (near[:, k : k + 1] < 1792).astype(F32)
        incoming = (total * gain[...]).astype(BF16)
        both = jnp.concatenate([own, incoming], axis=1)
        node = jnp.maximum(dot(both, node_in[...]) + node_bias[...], 0.0).astype(BF16)
        new_out[here, :] = own.astype(F32) + normed(dot(node, node_out[...])) * node_gain[...]
        return carry

    lax.fori_loop(0, blocks, step, 0)


def columns_of(slots):
    places = slots[...]
    return jnp.concatenate([jnp.broadcast_to(places[:, k : k + 1], (16, 128)) for k in range(64)], axis=0)


def found_in(column, sources):
    lane = lax.broadcasted_iota(jnp.int32, (1024, 128), 1)
    total = jnp.zeros((1024, D), F32)
    for start, source in sources:
        picked = [
            (column == lane + (start + t * 128)).astype(F32).astype(BF16) for t in range(source.shape[0] // 128)
        ]
        total = total + dot(jnp.concatenate(picked, axis=1), source[...])
    return total


def gather_kernel(slots, m0, m1, m2, m3, m4, found_out):
    sources = ((0, m0), (512, m1), (1024, m2), (1536, m3), (1792, m4))
    found_out[...] = found_in(columns_of(slots), sources).astype(BF16)


def coarse_kernel(
    found, o0, o1, o2, o3, o4, slots, pool, medium, comp, member, *rest,
):
    *news, edge_in, edge_bias, edge_out, edge_gain, node_in, node_bias, node_out, node_gain, fine_out, medium_out, coarse_out = rest
    pool_rows = pool[...]
    received = dot(pool_rows, edge_in[...]) + edge_bias[...]
    sources = ((2048, o0), (2560, o1), (3072, o2), (3584, o3), (3840, o4))
    total = found[...].astype(F32) + found_in(columns_of(slots), sources)
    hidden = jnp.maximum(total.reshape(64, 16, D) + received[None], 0.0).astype(BF16).reshape(1024, D)
    message = normed(dot(hidden, edge_out[...])) * edge_gain[...]
    incoming = jnp.sum(message.reshape(64, 16, D), axis=0).astype(BF16)
    both = jnp.concatenate([pool_rows, incoming], axis=1)
    hidden = jnp.maximum(dot(both, node_in[...]) + node_bias[...], 0.0).astype(BF16)
    delta = normed(dot(hidden, node_out[...])) * node_gain[...]
    coarse_out[...] = (pool_rows.astype(F32) + delta).astype(BF16)
    high = delta.astype(BF16)
    low = (delta - high.astype(F32)).astype(BF16)
    parts = jnp.concatenate([high, low], axis=0)
    medium_out[...] = (medium[...] + dot_t(member[...], parts)).astype(BF16)
    spread = dot_t(comp[...], parts)
    first = 0
    for new in news:
        last = first + new.shape[0]
        fine_out[first:last, :] = (new[...] + spread[first:last]).astype(BF16)
        first = last


def joined(*parts):
    return jnp.concatenate(parts, axis=0)


def sent(rows, pairs):
    return lax.ppermute(rows, AXES, pairs)


def local(
    fine_state, fine_nbrs, send_rows, ghost_counts, fine_parent, medium_state, medium_parent, coarse_state,
    coarse_nbrs, fine_edge_in, fine_edge_bias, fine_edge_out, fine_edge_gain, fine_node_in, fine_node_bias,
    fine_node_out, fine_node_gain, coarse_edge_in, coarse_edge_bias, coarse_edge_out, coarse_edge_gain,
    coarse_node_in, coarse_node_bias, coarse_node_out, coarse_node_gain,
):
    row = lambda vector: vector.reshape(1, -1)
    shaped = jax.ShapeDtypeStruct
    held = pl.BlockSpec(memory_space=pltpu.VMEM)
    far = pl.BlockSpec(memory_space=pltpu.HBM)
    scalars = pl.BlockSpec(memory_space=pltpu.SMEM)
    upper = pl.BlockSpec((D, D), lambda i: (1, 0), memory_space=pltpu.VMEM)
    tied = lax.optimization_barrier
    distant = functools.partial(pltpu.with_memory_space_constraint, memory_space=pltpu.HBM)

    def kernel(body, outs, specs, args, scratch=(), limit=32, cost=None):
        return pl.pallas_call(
            body,
            grid=(1,),
            out_shape=outs,
            in_specs=specs,
            out_specs=[held] * len(outs),
            scratch_shapes=list(scratch),
            compiler_params=pltpu.CompilerParams(vmem_limit_bytes=limit << 20),
            cost_estimate=cost,
        )(*args)

    sender, pool, medium_pool, slots, comp, member = kernel(
        pool_kernel,
        [
            shaped((16, D), BF16),
            shaped((16, D), BF16),
            shaped((128, D), F32),
            shaped((16, 64), jnp.int32),
            shaped((32, 1024), BF16),
            shaped((32, 128), BF16),
        ],
        [far] * 7,
        [
            distant(value)
            for value in (
                fine_state, row(fine_parent), medium_state, row(medium_parent), coarse_state, coarse_nbrs,
                coarse_edge_in,
            )
        ],
        [
            pltpu.VMEM((1024, D), BF16),
            pltpu.VMEM((1, 1024), jnp.int32),
            pltpu.VMEM((128, D), BF16),
            pltpu.VMEM((1, 128), jnp.int32),
            pltpu.VMEM((16, D), BF16),
            pltpu.VMEM((16, 64), jnp.int32),
            pltpu.VMEM((D, D), BF16),
            pltpu.SemaphoreType.DMA((7,)),
        ],
    )
    fine_sender, centred, *faces = kernel(
        face_kernel,
        [shaped((1024, D), BF16), shaped((D, D), BF16)] + [shaped((1, 128, D), BF16)] * 6,
        [pl.BlockSpec(memory_space=pl.ANY), far, far, scalars, far, far],
        (
            member, distant(fine_state), distant(send_rows.reshape(1, 768)), ghost_counts, distant(fine_edge_in),
            distant(fine_edge_out),
        ),
        [
            pltpu.VMEM((1024, D), BF16),
            pltpu.VMEM((1, 768), jnp.int32),
            pltpu.VMEM((D, D), BF16),
            pltpu.VMEM((D, D), BF16),
            pltpu.SemaphoreType.DMA((4,)),
        ],
    )

    def faced(face):
        axes = (("x", "zh", "c"), "y")[face // 2]
        count = lax.axis_size(axes)
        pairs = [(k, k + 1) for k in range(count - 1)]
        return lax.ppermute(faces[face], axes, [(b, a) for a, b in pairs] if face % 2 == 0 else pairs)

    ups, downs = [sent(sender, UP_Z)], [sent(sender, DOWN_Z)]
    up, down, faces[5], faces[4], faces[1] = tied((ups[-1], downs[-1], faces[5], faces[4], faces[1]))
    ups.append(sent(up, UP_Z))
    downs.append(sent(down, DOWN_Z))
    low_x, low_z, high_z = faced(1), sent(faces[5], UP_Z), sent(faces[4], DOWN_Z)
    up, down, faces[0] = tied((ups[-1], downs[-1], faces[0]))
    ups.append(sent(up, UP_Z))
    downs.append(sent(down, DOWN_Z))
    high_x = faced(0)
    up, down, faces[3], faces[2], low_x = tied((ups[-1], downs[-1], faces[3], faces[2], low_x))
    ups.append(sent(up, UP_Z))
    low_y, high_y = faced(3), faced(2)
    last, high_x = tied((ups[-1], high_x))
    column = joined(sender, *ups[:3], last, *downs)
    near_faces = [low_x, high_x, low_y, high_y, low_z, high_z]
    fine_sender, column = tied((fine_sender, column))
    table, near = kernel(
        table_kernel,
        [shaped((1792, D), BF16), shaped((1024, 8), jnp.int32)],
        [pl.BlockSpec(memory_space=pl.ANY)] * 7 + [held],
        (fine_sender, *near_faces, fine_nbrs.T),
        [pltpu.SemaphoreType.DMA((7,))],
    )
    news = []

    def edges(blocks):
        first = sum(new.shape[0] for new in news) // BLOCK
        news.extend(
            kernel(
                functools.partial(edge_kernel, first=first),
                [shaped((blocks * BLOCK, D), F32)],
                [held] * 3 + [upper] + [held] * 7,
                (
                    table, fine_state, near, fine_edge_in, row(fine_edge_bias), centred, row(fine_edge_gain),
                    fine_node_in, row(fine_node_bias), fine_node_out, row(fine_node_gain),
                ),
                [pltpu.VMEM((6 * BLOCK, 1792), BF16), pltpu.VMEM((6 * BLOCK, D), BF16)],
                cost=pl.CostEstimate(
                    flops=blocks * 1_700_000_000, bytes_accessed=blocks * 3_000_000, transcendentals=0
                ),
            )
        )

    up, down = sent(column, UP_FIRST), sent(column, DOWN_FIRST)
    edges(SHARES[0])
    up, down, news[-1] = tied((up, down, news[-1]))
    table, up = tied((table, up))
    rest = [sent(up[:64], UP_FIRST), sent(down[64:], DOWN_FIRST)]
    edges(SHARES[1])
    *rest, news[-1] = tied((*rest, news[-1]))
    line = joined(column, up, down, *rest)
    table, line = tied((table, line))
    up, down = sent(line, UP_SECOND), sent(line, DOWN_SECOND)
    others = [sent(line, SWAP)]
    edges(SHARES[2])
    up, down, news[-1] = tied((up, down, news[-1]))
    table, up = tied((table, up))
    rest = [sent(up[:256], UP_SECOND), sent(down[256:], DOWN_SECOND)]
    others += [sent(up, SWAP), sent(down, SWAP)]
    edges(SHARES[3])
    *rest, news[-1] = tied((*rest, news[-1]))
    others += [sent(part, SWAP) for part in rest]
    (found,) = kernel(
        gather_kernel, [shaped((1024, D), BF16)], [held] * 6, (slots, line, up, down, *rest), limit=40,
        cost=pl.CostEstimate(flops=2_000_000_000, bytes_accessed=4_000_000, transcendentals=0),
    )
    fine_out, medium_out, coarse_out = kernel(
        coarse_kernel,
        [shaped((1024, D), BF16), shaped((128, D), BF16), shaped((16, D), BF16)],
        [held] * (11 + len(news)) + [upper] + [held] * 7,
        (
            found, *others, slots, pool, medium_pool, comp, member, *news, coarse_edge_in, row(coarse_edge_bias),
            coarse_edge_out, row(coarse_edge_gain), coarse_node_in, row(coarse_node_bias), coarse_node_out,
            row(coarse_node_gain),
        ),
        limit=48,
    )
    return fine_out, medium_out, coarse_out


def solution(mesh):
    torus = Mesh(mesh.devices.reshape(SIZES), AXES)
    rows = P(AXES, None)
    placed = (rows, rows, P(AXES, None, None), rows, P(AXES), rows, P(AXES), rows, rows) + (P(),) * 16
    return jax.shard_map(local, mesh=torus, in_specs=placed, out_specs=(rows, rows, rows), check_vma=False)
```

```python
import functools
import itertools

import jax
import jax.numpy as jnp
from jax import lax
from jax.experimental import pallas as pl
from jax.experimental.pallas import tpu as pltpu
from jax.sharding import Mesh
from jax.sharding import PartitionSpec as P

AXES = ("x", "zh", "c", "y", "z")
SIZES = (4, 2, 2, 4, 4)
EPS = 1e-05
F32 = jnp.float32
BF16 = jnp.bfloat16
D = 512
BLOCK = 128
SHARES = (3, 3, 2)


def linear(place):
    number = 0
    for size, at in zip(SIZES, place):
        number = number * size + at
    return number


def permutation(move):
    pairs = []
    for place in itertools.product(*(range(size) for size in SIZES)):
        target = move(*place)
        if target is not None:
            pairs.append((linear(place), linear(target)))
    return pairs


def along_z(x, zh, c, y, z, step):
    at = (zh * 4 + z + step) % 8
    return (x, at // 4, c, y, at % 4)


def along_plane(x, zh, c, y, z, step, first):
    if (c == 0) == first:
        return ((x + step) % 4, zh, c, y, z)
    return (x, zh, c, (y + step) % 4, z)


SWAP = permutation(lambda x, zh, c, y, z: (x, zh, 1 - c, y, z))
UP_Z = permutation(functools.partial(along_z, step=1))
DOWN_Z = permutation(functools.partial(along_z, step=-1))
UP_3Z = permutation(functools.partial(along_z, step=3))
DOWN_3Z = permutation(functools.partial(along_z, step=-3))
UP_FIRST = permutation(functools.partial(along_plane, step=1, first=True))
DOWN_FIRST = permutation(functools.partial(along_plane, step=-1, first=True))
UP_SECOND = permutation(functools.partial(along_plane, step=1, first=False))
DOWN_SECOND = permutation(functools.partial(along_plane, step=-1, first=False))


def dot(a, b):
    return lax.dot_general(a, b, (((1,), (0,)), ((), ())), preferred_element_type=F32)


def dot_t(a, b):
    return lax.dot_general(a, b, (((0,), (0,)), ((), ())), preferred_element_type=F32)


def normed(values):
    center = values - jnp.mean(values, axis=-1, keepdims=True)
    spread = jnp.mean(center * center, axis=-1, keepdims=True)
    return center * lax.rsqrt(spread + EPS)


def pool_kernel(
    fine_h, parent_h, medium_h, medium_parent_h, coarse_h, nbrs_h, weight_h,
    sender_out, pool_out, medium_out, slots_out, comp_out, member_out,
    fine, parent, medium, medium_parent, coarse, nbrs, weight, sems,
):
    pairs = (
        (parent_h, parent), (fine_h, fine), (medium_h, medium), (medium_parent_h, medium_parent),
        (coarse_h, coarse), (weight_h.at[pl.ds(0, D)], weight), (nbrs_h, nbrs),
    )
    copies = [pltpu.make_async_copy(source, target, sems.at[k]) for k, (source, target) in enumerate(pairs)]
    for copy in copies:
        copy.start()
    for copy in copies:
        copy.wait()
    member = (parent[...] == lax.broadcasted_iota(jnp.int32, (128, 1024), 0)).astype(F32)
    count = jnp.sum(member, axis=1, keepdims=True)
    member = member.astype(BF16)
    medium_pool = medium[...].astype(F32) + dot(member, fine[...]) / count
    medium_out[...] = medium_pool
    upper = (medium_parent[...] == lax.broadcasted_iota(jnp.int32, (16, 128), 0)).astype(F32)
    upper_count = jnp.sum(upper, axis=1, keepdims=True)
    total = jnp.dot(upper, medium_pool, precision=lax.Precision.HIGHEST, preferred_element_type=F32)
    pool = (coarse[...].astype(F32) + total / upper_count).astype(BF16)
    pool_out[...] = pool
    sender_out[...] = dot(pool, weight[...]).astype(BF16)
    upper = upper.astype(BF16)
    member_out[...] = jnp.concatenate([upper, upper], axis=0)
    comp = dot(upper, member).astype(BF16)
    comp_out[...] = jnp.concatenate([comp, comp], axis=0)
    here = {name: lax.axis_index(name) for name in AXES}
    row = nbrs[...] & 15
    owner = nbrs[...] >> 4
    z = owner & 3
    y = (owner >> 2) & 3
    c = (owner >> 4) & 1
    zh = (owner >> 5) & 1
    x = owner >> 6
    back = (here["zh"] * 4 + here["z"] - zh * 4 - z) & 7
    stream = c
    at = ((back + 1) & 7) * 16 + row
    step_x = (here["x"] - x) & 3
    step_y = (here["y"] - y) & 3
    order_x = jnp.where(step_x == 2, 3, jnp.where(step_x == 3, 2, step_x))
    order_y = jnp.where(step_y == 2, 3, jnp.where(step_y == 3, 2, step_y))
    at = at + jnp.where(stream == 0, order_x * 128 + order_y * 512, order_y * 128 + order_x * 512)
    slots_out[...] = at + jnp.where(stream == here["c"], 0, 2048)


def face_kernel(
    pool, fine_h, rows_h, counts, weight_h, edge_out_h, coarse_in_h, coarse_bias,
    sender_out, centred_out, received_out, f0, f1, f2, f3, f4, f5,
    fine, rows, weight, edge_out, coarse_in, sems,
):
    pairs = (
        (rows_h, rows), (fine_h, fine), (weight_h.at[pl.ds(0, D)], weight), (edge_out_h, edge_out),
        (coarse_in_h.at[pl.ds(D, D)], coarse_in),
    )
    copies = [pltpu.make_async_copy(source, target, sems.at[k]) for k, (source, target) in enumerate(pairs)]
    for copy in copies:
        copy.start()
    for copy in copies:
        copy.wait()
    sender = dot(fine[...], weight[...]).astype(BF16)
    sender_out[...] = sender
    received_out[...] = dot(pool[...], coarse_in[...]) + coarse_bias[...]
    wide = edge_out[...].astype(F32)
    centred_out[...] = (wide - jnp.mean(wide, axis=1, keepdims=True)).astype(BF16)
    flat = jnp.concatenate(
        [rows[:, 128 * face : 128 * (face + 1)] for face in range(6)] + [jnp.zeros((2, 128), jnp.int32)], axis=0
    )
    columns = flat.T
    place = lax.broadcasted_iota(jnp.int32, (128, 1), 0)
    for face, face_out in enumerate((f0, f1, f2, f3, f4, f5)):
        wanted = jnp.where(place < counts[0, face], columns[:, face : face + 1], -1)
        picked = (wanted == lax.broadcasted_iota(jnp.int32, (128, 1024), 1)).astype(F32).astype(BF16)
        face_out[0] = dot(picked, sender).astype(BF16)


def table_kernel(sender, g0, g1, g2, g3, g4, g5, nbrs, table_out, near_out, sems):
    copies = [pltpu.make_async_copy(sender, table_out.at[pl.ds(0, 1024)], sems.at[0])]
    for k, ghost in enumerate((g0, g1, g2, g3, g4, g5)):
        copies.append(
            pltpu.make_async_copy(ghost.at[0], table_out.at[pl.ds(1024 + 128 * k, 128)], sems.at[1 + k])
        )
    for copy in copies:
        copy.start()
    padded = jnp.concatenate([nbrs[...], jnp.zeros((2, 1024), jnp.int32)], axis=0)
    for block in range(8):
        near_out[block * 128 : (block + 1) * 128, :] = padded[:, block * 128 : (block + 1) * 128].T
    for copy in copies:
        copy.wait()


def edge_kernel(
    table, fine, nbrs, receive, bias, centred, gain, node_in, node_bias, node_out, node_gain,
    new_out,
    picked, hidden,
    *, first,
):
    blocks = new_out.shape[0] // BLOCK

    def step(block, carry):
        here = pl.ds(pl.multiple_of(block * BLOCK, BLOCK), BLOCK)
        span = pl.ds(pl.multiple_of((first + block) * BLOCK, BLOCK), BLOCK)
        own = fine[span, :]
        near = nbrs[span, :]
        received = dot(own, receive[...]) + bias[...]
        for k in range(6):
            wanted = near[:, k : k + 1]
            match = wanted == lax.broadcasted_iota(jnp.int32, (BLOCK, 1792), 1)
            picked[k * BLOCK : (k + 1) * BLOCK, :] = match.astype(F32).astype(BF16)
        found = dot(picked[...], table[...]).astype(BF16).astype(F32)
        hidden[...] = jnp.maximum(found + jnp.concatenate([received] * 6, axis=0), 0.0).astype(BF16)
        out = dot(hidden[...], centred[...])
        out = out * lax.rsqrt(jnp.mean(out * out, axis=-1, keepdims=True) + EPS)
        total = jnp.zeros((BLOCK, D), F32)
        for k in range(6):
            total = total + out[k * BLOCK : (k + 1) * BLOCK] * (near[:, k : k + 1] < 1792).astype(F32)
        incoming = (total * gain[...]).astype(BF16)
        both = jnp.concatenate([own, incoming], axis=1)
        node = jnp.maximum(dot(both, node_in[...]) + node_bias[...], 0.0).astype(BF16)
        new_out[here, :] = own.astype(F32) + normed(dot(node, node_out[...])) * node_gain[...]
        return carry

    lax.fori_loop(0, blocks, step, 0)


def columns_of(slots):
    places = slots[...]
    return jnp.concatenate([jnp.broadcast_to(places[:, k : k + 1], (16, 128)) for k in range(64)], axis=0)


def found_in(column, sources):
    lane = lax.broadcasted_iota(jnp.int32, (1024, 128), 1)
    total = jnp.zeros((1024, D), F32)
    for start, source in sources:
        picked = [
            (column == lane + (start + t * 128)).astype(F32).astype(BF16) for t in range(source.shape[0] // 128)
        ]
        total = total + dot(jnp.concatenate(picked, axis=1), source[...])
    return total


def gather_kernel(slots, m0, m1, m2, m3, m4, found_out):
    sources = ((0, m0), (512, m1), (1024, m2), (1536, m3), (1792, m4))
    found_out[...] = found_in(columns_of(slots), sources).astype(BF16)


def coarse_kernel(
    found, o0, o1, o2, o3, o4, slots, pool, medium, comp, member, *rest,
):
    *news, received, edge_out, edge_gain, node_in, node_bias, node_out, node_gain, fine_out, medium_out, coarse_out = rest
    pool_rows = pool[...]
    sources = ((2048, o0), (2560, o1), (3072, o2), (3584, o3), (3840, o4))
    total = found[...].astype(F32) + found_in(columns_of(slots), sources)
    hidden = jnp.maximum(total.reshape(64, 16, D) + received[...][None], 0.0).astype(BF16).reshape(1024, D)
    message = normed(dot(hidden, edge_out[...])) * edge_gain[...]
    incoming = jnp.sum(message.reshape(64, 16, D), axis=0).astype(BF16)
    both = jnp.concatenate([pool_rows, incoming], axis=1)
    hidden = jnp.maximum(dot(both, node_in[...]) + node_bias[...], 0.0).astype(BF16)
    delta = normed(dot(hidden, node_out[...])) * node_gain[...]
    coarse_out[...] = (pool_rows.astype(F32) + delta).astype(BF16)
    high = delta.astype(BF16)
    low = (delta - high.astype(F32)).astype(BF16)
    parts = jnp.concatenate([high, low], axis=0)
    medium_out[...] = (medium[...] + dot_t(member[...], parts)).astype(BF16)
    spread = dot_t(comp[...], parts)
    first = 0
    for new in news:
        last = first + new.shape[0]
        fine_out[first:last, :] = (new[...] + spread[first:last]).astype(BF16)
        first = last


def joined(*parts):
    return jnp.concatenate(parts, axis=0)


def sent(rows, pairs):
    return lax.ppermute(rows, AXES, pairs)


def local(
    fine_state, fine_nbrs, send_rows, ghost_counts, fine_parent, medium_state, medium_parent, coarse_state,
    coarse_nbrs, fine_edge_in, fine_edge_bias, fine_edge_out, fine_edge_gain, fine_node_in, fine_node_bias,
    fine_node_out, fine_node_gain, coarse_edge_in, coarse_edge_bias, coarse_edge_out, coarse_edge_gain,
    coarse_node_in, coarse_node_bias, coarse_node_out, coarse_node_gain,
):
    row = lambda vector: vector.reshape(1, -1)
    shaped = jax.ShapeDtypeStruct
    held = pl.BlockSpec(memory_space=pltpu.VMEM)
    far = pl.BlockSpec(memory_space=pltpu.HBM)
    scalars = pl.BlockSpec(memory_space=pltpu.SMEM)
    upper = pl.BlockSpec((D, D), lambda i: (1, 0), memory_space=pltpu.VMEM)
    tied = lax.optimization_barrier
    distant = functools.partial(pltpu.with_memory_space_constraint, memory_space=pltpu.HBM)

    def kernel(body, outs, specs, args, scratch=(), limit=32, cost=None):
        return pl.pallas_call(
            body,
            grid=(1,),
            out_shape=outs,
            in_specs=specs,
            out_specs=[held] * len(outs),
            scratch_shapes=list(scratch),
            compiler_params=pltpu.CompilerParams(vmem_limit_bytes=limit << 20),
            cost_estimate=cost,
        )(*args)

    sender, pool, medium_pool, slots, comp, member = kernel(
        pool_kernel,
        [
            shaped((16, D), BF16),
            shaped((16, D), BF16),
            shaped((128, D), F32),
            shaped((16, 64), jnp.int32),
            shaped((32, 1024), BF16),
            shaped((32, 128), BF16),
        ],
        [far] * 7,
        [
            distant(value)
            for value in (
                fine_state, row(fine_parent), medium_state, row(medium_parent), coarse_state, coarse_nbrs,
                coarse_edge_in,
            )
        ],
        [
            pltpu.VMEM((1024, D), BF16),
            pltpu.VMEM((1, 1024), jnp.int32),
            pltpu.VMEM((128, D), BF16),
            pltpu.VMEM((1, 128), jnp.int32),
            pltpu.VMEM((16, D), BF16),
            pltpu.VMEM((16, 64), jnp.int32),
            pltpu.VMEM((D, D), BF16),
            pltpu.SemaphoreType.DMA((7,)),
        ],
    )
    fine_sender, centred, received, *faces = kernel(
        face_kernel,
        [shaped((1024, D), BF16), shaped((D, D), BF16), shaped((16, D), F32)] + [shaped((1, 128, D), BF16)] * 6,
        [held, far, far, scalars, far, far, far, held],
        (
            pool, distant(fine_state), distant(send_rows.reshape(1, 768)), ghost_counts, distant(fine_edge_in),
            distant(fine_edge_out), distant(coarse_edge_in), row(coarse_edge_bias),
        ),
        [
            pltpu.VMEM((1024, D), BF16),
            pltpu.VMEM((1, 768), jnp.int32),
            pltpu.VMEM((D, D), BF16),
            pltpu.VMEM((D, D), BF16),
            pltpu.VMEM((D, D), BF16),
            pltpu.SemaphoreType.DMA((5,)),
        ],
    )

    def faced(face):
        axes = (("x", "zh", "c"), "y")[face // 2]
        count = lax.axis_size(axes)
        pairs = [(k, k + 1) for k in range(count - 1)]
        return lax.ppermute(faces[face], axes, [(b, a) for a, b in pairs] if face % 2 == 0 else pairs)

    low, high = sent(sender, UP_Z), sent(sender, DOWN_Z)
    low, high, faces[0], faces[1] = tied((low, high, faces[0], faces[1]))
    three = joined(high, sender, low)
    lower, higher = sent(three, UP_3Z), sent(three[16:], DOWN_3Z)
    low_x, high_x = faced(1), faced(0)
    lower, higher, *faces[2:] = tied((lower, higher, *faces[2:]))
    column = joined(three, lower, higher)
    up, down = sent(column, UP_FIRST), sent(column, DOWN_FIRST)
    low_y, high_y = faced(3), faced(2)
    low_z, high_z = sent(faces[5], UP_Z), sent(faces[4], DOWN_Z)
    up, down, low_x, high_x = tied((up, down, low_x, high_x))
    near_faces = [low_x, high_x, low_y, high_y, low_z, high_z]
    table, near = kernel(
        table_kernel,
        [shaped((1792, D), BF16), shaped((1024, 8), jnp.int32)],
        [pl.BlockSpec(memory_space=pl.ANY)] * 7 + [held],
        (fine_sender, *near_faces, fine_nbrs.T),
        [pltpu.SemaphoreType.DMA((7,))],
    )
    news = []

    def edges(blocks):
        first = sum(new.shape[0] for new in news) // BLOCK
        news.extend(
            kernel(
                functools.partial(edge_kernel, first=first),
                [shaped((blocks * BLOCK, D), F32)],
                [held] * 3 + [upper] + [held] * 7,
                (
                    table, fine_state, near, fine_edge_in, row(fine_edge_bias), centred, row(fine_edge_gain),
                    fine_node_in, row(fine_node_bias), fine_node_out, row(fine_node_gain),
                ),
                [pltpu.VMEM((6 * BLOCK, 1792), BF16), pltpu.VMEM((6 * BLOCK, D), BF16)],
                cost=pl.CostEstimate(
                    flops=blocks * 1_700_000_000, bytes_accessed=blocks * 3_000_000, transcendentals=0
                ),
            )
        )

    rest = [sent(up[:64], UP_FIRST), sent(down[64:], DOWN_FIRST)]
    line = joined(column, up, down, *rest)
    table, line = tied((table, line))
    up, down = sent(line, UP_SECOND), sent(line, DOWN_SECOND)
    others = [sent(line, SWAP)]
    edges(SHARES[0])
    up, down, news[-1] = tied((up, down, news[-1]))
    table, up = tied((table, up))
    rest = [sent(up[:256], UP_SECOND), sent(down[256:], DOWN_SECOND)]
    others += [sent(up, SWAP), sent(down, SWAP)]
    edges(SHARES[1])
    *rest, news[-1] = tied((*rest, news[-1]))
    table, rest[0] = tied((table, rest[0]))
    others += [sent(part, SWAP) for part in rest]
    edges(SHARES[2])
    (found,) = kernel(
        gather_kernel, [shaped((1024, D), BF16)], [held] * 6, (slots, line, up, down, *rest), limit=40,
        cost=pl.CostEstimate(flops=2_000_000_000, bytes_accessed=4_000_000, transcendentals=0),
    )
    fine_out, medium_out, coarse_out = kernel(
        coarse_kernel,
        [shaped((1024, D), BF16), shaped((128, D), BF16), shaped((16, D), BF16)],
        [held] * (18 + len(news)),
        (
            found, *others, slots, pool, medium_pool, comp, member, *news, received,
            coarse_edge_out, row(coarse_edge_gain), coarse_node_in, row(coarse_node_bias), coarse_node_out,
            row(coarse_node_gain),
        ),
        limit=48,
    )
    return fine_out, medium_out, coarse_out


def solution(mesh):
    torus = Mesh(mesh.devices.reshape(SIZES), AXES)
    rows = P(AXES, None)
    placed = (rows, rows, P(AXES, None, None), rows, P(AXES), rows, P(AXES), rows, rows) + (P(),) * 16
    return jax.shard_map(local, mesh=torus, in_specs=placed, out_specs=(rows, rows, rows), check_vma=False)
```

```python
import functools
import itertools

import jax
import jax.numpy as jnp
from jax import lax
from jax.experimental import pallas as pl
from jax.experimental.pallas import tpu as pltpu
from jax.sharding import Mesh
from jax.sharding import PartitionSpec as P

AXES = ("x", "zh", "c", "y", "z")
SIZES = (4, 2, 2, 4, 4)
EPS = 1e-05
F32 = jnp.float32
BF16 = jnp.bfloat16
D = 512
BLOCK = 128
SHARES = (3, 3, 2)


def linear(place):
    number = 0
    for size, at in zip(SIZES, place):
        number = number * size + at
    return number


def permutation(move):
    pairs = []
    for place in itertools.product(*(range(size) for size in SIZES)):
        target = move(*place)
        if target is not None:
            pairs.append((linear(place), linear(target)))
    return pairs


def along_z(x, zh, c, y, z, step):
    at = (zh * 4 + z + step) % 8
    return (x, at // 4, c, y, at % 4)


def along_plane(x, zh, c, y, z, step, first):
    if (c == 0) == first:
        return ((x + step) % 4, zh, c, y, z)
    return (x, zh, c, (y + step) % 4, z)


SWAP = permutation(lambda x, zh, c, y, z: (x, zh, 1 - c, y, z))
UP_Z = permutation(functools.partial(along_z, step=1))
DOWN_Z = permutation(functools.partial(along_z, step=-1))
UP_3Z = permutation(functools.partial(along_z, step=3))
DOWN_3Z = permutation(functools.partial(along_z, step=-3))
UP_FIRST = permutation(functools.partial(along_plane, step=1, first=True))
DOWN_FIRST = permutation(functools.partial(along_plane, step=-1, first=True))
UP_SECOND = permutation(functools.partial(along_plane, step=1, first=False))
DOWN_SECOND = permutation(functools.partial(along_plane, step=-1, first=False))


def dot(a, b):
    return lax.dot_general(a, b, (((1,), (0,)), ((), ())), preferred_element_type=F32)


def dot_t(a, b):
    return lax.dot_general(a, b, (((0,), (0,)), ((), ())), preferred_element_type=F32)


def normed(values):
    center = values - jnp.mean(values, axis=-1, keepdims=True)
    spread = jnp.mean(center * center, axis=-1, keepdims=True)
    return center * lax.rsqrt(spread + EPS)


def pool_kernel(
    fine_h, parent_h, medium_h, medium_parent_h, coarse_h, nbrs_h, weight_h,
    sender_out, pool_out, medium_out, slots_out, comp_out, member_out,
    fine, parent, medium, medium_parent, coarse, nbrs, weight, sems,
):
    pairs = (
        (parent_h, parent), (fine_h, fine), (medium_h, medium), (medium_parent_h, medium_parent),
        (coarse_h, coarse), (weight_h.at[pl.ds(0, D)], weight), (nbrs_h, nbrs),
    )
    copies = [pltpu.make_async_copy(source, target, sems.at[k]) for k, (source, target) in enumerate(pairs)]
    for copy in copies:
        copy.start()
    for copy in copies:
        copy.wait()
    member = (parent[...] == lax.broadcasted_iota(jnp.int32, (128, 1024), 0)).astype(F32)
    count = jnp.sum(member, axis=1, keepdims=True)
    member = member.astype(BF16)
    medium_pool = medium[...].astype(F32) + dot(member, fine[...]) / count
    medium_out[...] = medium_pool
    upper = (medium_parent[...] == lax.broadcasted_iota(jnp.int32, (16, 128), 0)).astype(F32)
    upper_count = jnp.sum(upper, axis=1, keepdims=True)
    total = jnp.dot(upper, medium_pool, precision=lax.Precision.HIGHEST, preferred_element_type=F32)
    pool = (coarse[...].astype(F32) + total / upper_count).astype(BF16)
    pool_out[...] = pool
    sender_out[...] = dot(pool, weight[...]).astype(BF16)
    upper = upper.astype(BF16)
    member_out[...] = jnp.concatenate([upper, upper], axis=0)
    comp = dot(upper, member).astype(BF16)
    comp_out[...] = jnp.concatenate([comp, comp], axis=0)
    here = {name: lax.axis_index(name) for name in AXES}
    row = nbrs[...] & 15
    owner = nbrs[...] >> 4
    z = owner & 3
    y = (owner >> 2) & 3
    c = (owner >> 4) & 1
    zh = (owner >> 5) & 1
    x = owner >> 6
    back = (here["zh"] * 4 + here["z"] - zh * 4 - z) & 7
    stream = c
    at = ((back + 1) & 7) * 16 + row
    step_x = (here["x"] - x) & 3
    step_y = (here["y"] - y) & 3
    order_x = jnp.where(step_x == 2, 3, jnp.where(step_x == 3, 2, step_x))
    order_y = jnp.where(step_y == 2, 3, jnp.where(step_y == 3, 2, step_y))
    at = at + jnp.where(stream == 0, order_x * 128 + order_y * 512, order_y * 128 + order_x * 512)
    slots_out[...] = at + jnp.where(stream == here["c"], 0, 2048)


def face_kernel(
    pool, fine_h, rows_h, counts, weight_h, edge_out_h, coarse_in_h, coarse_bias,
    sender_out, centred_out, received_out, f0, f1, f2, f3, f4, f5,
    fine, rows, weight, edge_out, coarse_in, sems,
):
    pairs = (
        (rows_h, rows), (fine_h, fine), (weight_h.at[pl.ds(0, D)], weight), (edge_out_h, edge_out),
        (coarse_in_h.at[pl.ds(D, D)], coarse_in),
    )
    copies = [pltpu.make_async_copy(source, target, sems.at[k]) for k, (source, target) in enumerate(pairs)]
    for copy in copies:
        copy.start()
    for copy in copies:
        copy.wait()
    sender = dot(fine[...], weight[...]).astype(BF16)
    sender_out[...] = sender
    received_out[...] = dot(pool[...], coarse_in[...]) + coarse_bias[...]
    wide = edge_out[...].astype(F32)
    centred_out[...] = (wide - jnp.mean(wide, axis=1, keepdims=True)).astype(BF16)
    flat = jnp.concatenate(
        [rows[:, 128 * face : 128 * (face + 1)] for face in range(6)] + [jnp.zeros((2, 128), jnp.int32)], axis=0
    )
    columns = flat.T
    place = lax.broadcasted_iota(jnp.int32, (128, 1), 0)
    for face, face_out in enumerate((f0, f1, f2, f3, f4, f5)):
        wanted = jnp.where(place < counts[0, face], columns[:, face : face + 1], -1)
        picked = (wanted == lax.broadcasted_iota(jnp.int32, (128, 1024), 1)).astype(F32).astype(BF16)
        face_out[0] = dot(picked, sender).astype(BF16)


def table_kernel(sender, g0, g1, g2, g3, g4, g5, nbrs, table_out, near_out, sems):
    copies = [pltpu.make_async_copy(sender, table_out.at[pl.ds(0, 1024)], sems.at[0])]
    for k, ghost in enumerate((g0, g1, g2, g3, g4, g5)):
        copies.append(
            pltpu.make_async_copy(ghost.at[0], table_out.at[pl.ds(1024 + 128 * k, 128)], sems.at[1 + k])
        )
    for copy in copies:
        copy.start()
    padded = jnp.concatenate([nbrs[...], jnp.zeros((2, 1024), jnp.int32)], axis=0)
    for block in range(8):
        near_out[block * 128 : (block + 1) * 128, :] = padded[:, block * 128 : (block + 1) * 128].T
    for copy in copies:
        copy.wait()


def edge_kernel(
    table, fine, nbrs, receive, bias, centred, gain, node_in, node_bias, node_out, node_gain,
    new_out,
    picked, hidden,
    *, first,
):
    blocks = new_out.shape[0] // BLOCK

    def step(block, carry):
        here = pl.ds(pl.multiple_of(block * BLOCK, BLOCK), BLOCK)
        span = pl.ds(pl.multiple_of((first + block) * BLOCK, BLOCK), BLOCK)
        own = fine[span, :]
        near = nbrs[span, :]
        received = dot(own, receive[...]) + bias[...]
        for k in range(6):
            wanted = near[:, k : k + 1]
            match = wanted == lax.broadcasted_iota(jnp.int32, (BLOCK, 1792), 1)
            picked[k * BLOCK : (k + 1) * BLOCK, :] = match.astype(F32).astype(BF16)
        found = dot(picked[...], table[...]).astype(BF16).astype(F32)
        hidden[...] = jnp.maximum(found + jnp.concatenate([received] * 6, axis=0), 0.0).astype(BF16)
        out = dot(hidden[...], centred[...])
        out = out * lax.rsqrt(jnp.mean(out * out, axis=-1, keepdims=True) + EPS)
        total = jnp.zeros((BLOCK, D), F32)
        for k in range(6):
            total = total + out[k * BLOCK : (k + 1) * BLOCK] * (near[:, k : k + 1] < 1792).astype(F32)
        incoming = (total * gain[...]).astype(BF16)
        both = jnp.concatenate([own, incoming], axis=1)
        node = jnp.maximum(dot(both, node_in[...]) + node_bias[...], 0.0).astype(BF16)
        new_out[here, :] = own.astype(F32) + normed(dot(node, node_out[...])) * node_gain[...]
        return carry

    lax.fori_loop(0, blocks, step, 0)


def columns_of(slots):
    places = slots[...]
    return jnp.concatenate([jnp.broadcast_to(places[:, k : k + 1], (16, 128)) for k in range(64)], axis=0)


def found_in(column, sources):
    lane = lax.broadcasted_iota(jnp.int32, (1024, 128), 1)
    total = jnp.zeros((1024, D), F32)
    for start, source in sources:
        picked = [
            (column == lane + (start + t * 128)).astype(F32).astype(BF16) for t in range(source.shape[0] // 128)
        ]
        total = total + dot(jnp.concatenate(picked, axis=1), source[...])
    return total


def gather_kernel(slots, m0, m1, m2, m3, m4, found_out):
    sources = ((0, m0), (512, m1), (1024, m2), (1536, m3), (1792, m4))
    found_out[...] = found_in(columns_of(slots), sources).astype(BF16)


def coarse_kernel(
    found, o0, o1, o2, o3, o4, slots, pool, medium, comp, member, *rest,
):
    *news, received, edge_out, edge_gain, node_in, node_bias, node_out, node_gain, fine_out, medium_out, coarse_out = rest
    pool_rows = pool[...]
    sources = ((2048, o0), (2560, o1), (3072, o2), (3584, o3), (3840, o4))
    total = found[...].astype(F32) + found_in(columns_of(slots), sources)
    hidden = jnp.maximum(total.reshape(64, 16, D) + received[...][None], 0.0).astype(BF16).reshape(1024, D)
    message = normed(dot(hidden, edge_out[...])) * edge_gain[...]
    incoming = jnp.sum(message.reshape(64, 16, D), axis=0).astype(BF16)
    both = jnp.concatenate([pool_rows, incoming], axis=1)
    hidden = jnp.maximum(dot(both, node_in[...]) + node_bias[...], 0.0).astype(BF16)
    delta = normed(dot(hidden, node_out[...])) * node_gain[...]
    coarse_out[...] = (pool_rows.astype(F32) + delta).astype(BF16)
    high = delta.astype(BF16)
    low = (delta - high.astype(F32)).astype(BF16)
    parts = jnp.concatenate([high, low], axis=0)
    medium_out[...] = (medium[...] + dot_t(member[...], parts)).astype(BF16)
    spread = dot_t(comp[...], parts)
    first = 0
    for new in news:
        last = first + new.shape[0]
        fine_out[first:last, :] = (new[...] + spread[first:last]).astype(BF16)
        first = last


def joined(*parts):
    return jnp.concatenate(parts, axis=0)


def sent(rows, pairs):
    return lax.ppermute(rows, AXES, pairs)


def local(
    fine_state, fine_nbrs, send_rows, ghost_counts, fine_parent, medium_state, medium_parent, coarse_state,
    coarse_nbrs, fine_edge_in, fine_edge_bias, fine_edge_out, fine_edge_gain, fine_node_in, fine_node_bias,
    fine_node_out, fine_node_gain, coarse_edge_in, coarse_edge_bias, coarse_edge_out, coarse_edge_gain,
    coarse_node_in, coarse_node_bias, coarse_node_out, coarse_node_gain,
):
    row = lambda vector: vector.reshape(1, -1)
    shaped = jax.ShapeDtypeStruct
    held = pl.BlockSpec(memory_space=pltpu.VMEM)
    far = pl.BlockSpec(memory_space=pltpu.HBM)
    scalars = pl.BlockSpec(memory_space=pltpu.SMEM)
    upper = pl.BlockSpec((D, D), lambda i: (1, 0), memory_space=pltpu.VMEM)
    tied = lax.optimization_barrier
    distant = functools.partial(pltpu.with_memory_space_constraint, memory_space=pltpu.HBM)

    def kernel(body, outs, specs, args, scratch=(), limit=32, cost=None):
        return pl.pallas_call(
            body,
            grid=(1,),
            out_shape=outs,
            in_specs=specs,
            out_specs=[held] * len(outs),
            scratch_shapes=list(scratch),
            compiler_params=pltpu.CompilerParams(vmem_limit_bytes=limit << 20),
            cost_estimate=cost,
        )(*args)

    sender, pool, medium_pool, slots, comp, member = kernel(
        pool_kernel,
        [
            shaped((16, D), BF16),
            shaped((16, D), BF16),
            shaped((128, D), F32),
            shaped((16, 64), jnp.int32),
            shaped((32, 1024), BF16),
            shaped((32, 128), BF16),
        ],
        [far] * 7,
        [
            distant(value)
            for value in (
                fine_state, row(fine_parent), medium_state, row(medium_parent), coarse_state, coarse_nbrs,
                coarse_edge_in,
            )
        ],
        [
            pltpu.VMEM((1024, D), BF16),
            pltpu.VMEM((1, 1024), jnp.int32),
            pltpu.VMEM((128, D), BF16),
            pltpu.VMEM((1, 128), jnp.int32),
            pltpu.VMEM((16, D), BF16),
            pltpu.VMEM((16, 64), jnp.int32),
            pltpu.VMEM((D, D), BF16),
            pltpu.SemaphoreType.DMA((7,)),
        ],
    )
    fine_sender, centred, received, *faces = kernel(
        face_kernel,
        [shaped((1024, D), BF16), shaped((D, D), BF16), shaped((16, D), F32)] + [shaped((1, 128, D), BF16)] * 6,
        [held, far, far, scalars, far, far, far, held],
        (
            pool, distant(fine_state), distant(send_rows.reshape(1, 768)), ghost_counts, distant(fine_edge_in),
            distant(fine_edge_out), distant(coarse_edge_in), row(coarse_edge_bias),
        ),
        [
            pltpu.VMEM((1024, D), BF16),
            pltpu.VMEM((1, 768), jnp.int32),
            pltpu.VMEM((D, D), BF16),
            pltpu.VMEM((D, D), BF16),
            pltpu.VMEM((D, D), BF16),
            pltpu.SemaphoreType.DMA((5,)),
        ],
    )

    def faced(face):
        axes = (("x", "zh", "c"), "y")[face // 2]
        count = lax.axis_size(axes)
        pairs = [(k, k + 1) for k in range(count - 1)]
        return lax.ppermute(faces[face], axes, [(b, a) for a, b in pairs] if face % 2 == 0 else pairs)

    low, high = sent(sender, UP_Z), sent(sender, DOWN_Z)
    low, high, faces[0], faces[1] = tied((low, high, faces[0], faces[1]))
    three = joined(high, sender, low)
    lower, higher = sent(three, UP_3Z), sent(three[16:], DOWN_3Z)
    low_x, high_x = faced(1), faced(0)
    lower, higher, *faces[2:] = tied((lower, higher, *faces[2:]))
    column = joined(three, lower, higher)
    up, down = sent(column, UP_FIRST), sent(column, DOWN_FIRST)
    low_y, high_y = faced(3), faced(2)
    low_z, high_z = sent(faces[5], UP_Z), sent(faces[4], DOWN_Z)
    near_faces = [low_x, high_x, low_y, high_y, low_z, high_z]
    table, near = kernel(
        table_kernel,
        [shaped((1792, D), BF16), shaped((1024, 8), jnp.int32)],
        [pl.BlockSpec(memory_space=pl.ANY)] * 7 + [held],
        (fine_sender, *near_faces, fine_nbrs.T),
        [pltpu.SemaphoreType.DMA((7,))],
    )
    news = []

    def edges(blocks):
        first = sum(new.shape[0] for new in news) // BLOCK
        news.extend(
            kernel(
                functools.partial(edge_kernel, first=first),
                [shaped((blocks * BLOCK, D), F32)],
                [held] * 3 + [upper] + [held] * 7,
                (
                    table, fine_state, near, fine_edge_in, row(fine_edge_bias), centred, row(fine_edge_gain),
                    fine_node_in, row(fine_node_bias), fine_node_out, row(fine_node_gain),
                ),
                [pltpu.VMEM((6 * BLOCK, 1792), BF16), pltpu.VMEM((6 * BLOCK, D), BF16)],
                cost=pl.CostEstimate(
                    flops=blocks * 1_700_000_000, bytes_accessed=blocks * 3_000_000, transcendentals=0
                ),
            )
        )

    rest = [sent(up[:64], UP_FIRST), sent(down[64:], DOWN_FIRST)]
    line = joined(column, up, down, *rest)
    table, line = tied((table, line))
    up, down = sent(line, UP_SECOND), sent(line, DOWN_SECOND)
    others = [sent(line, SWAP)]
    edges(SHARES[0])
    up, down, news[-1] = tied((up, down, news[-1]))
    table, up = tied((table, up))
    rest = [sent(up[:256], UP_SECOND), sent(down[256:], DOWN_SECOND)]
    others += [sent(up, SWAP), sent(down, SWAP)]
    edges(SHARES[1])
    *rest, news[-1] = tied((*rest, news[-1]))
    table, rest[0] = tied((table, rest[0]))
    others += [sent(part, SWAP) for part in rest]
    edges(SHARES[2])
    (found,) = kernel(
        gather_kernel, [shaped((1024, D), BF16)], [held] * 6, (slots, line, up, down, *rest), limit=40,
        cost=pl.CostEstimate(flops=2_000_000_000, bytes_accessed=4_000_000, transcendentals=0),
    )
    fine_out, medium_out, coarse_out = kernel(
        coarse_kernel,
        [shaped((1024, D), BF16), shaped((128, D), BF16), shaped((16, D), BF16)],
        [held] * (18 + len(news)),
        (
            found, *others, slots, pool, medium_pool, comp, member, *news, received,
            coarse_edge_out, row(coarse_edge_gain), coarse_node_in, row(coarse_node_bias), coarse_node_out,
            row(coarse_node_gain),
        ),
        limit=48,
    )
    return fine_out, medium_out, coarse_out


def solution(mesh):
    torus = Mesh(mesh.devices.reshape(SIZES), AXES)
    rows = P(AXES, None)
    placed = (rows, rows, P(AXES, None, None), rows, P(AXES), rows, P(AXES), rows, rows) + (P(),) * 16
    return jax.shard_map(local, mesh=torus, in_specs=placed, out_specs=(rows, rows, rows), check_vma=False)
```

```python
import functools
import itertools

import jax
import jax.numpy as jnp
from jax import lax
from jax.experimental import pallas as pl
from jax.experimental.pallas import tpu as pltpu
from jax.sharding import Mesh
from jax.sharding import PartitionSpec as P

AXES = ("x", "zh", "c", "y", "z")
SIZES = (4, 2, 2, 4, 4)
EPS = 1e-05
F32 = jnp.float32
BF16 = jnp.bfloat16
D = 512
BLOCK = 128
SHARES = (4, 2, 2)


def linear(place):
    number = 0
    for size, at in zip(SIZES, place):
        number = number * size + at
    return number


def permutation(move):
    pairs = []
    for place in itertools.product(*(range(size) for size in SIZES)):
        target = move(*place)
        if target is not None:
            pairs.append((linear(place), linear(target)))
    return pairs


def along_z(x, zh, c, y, z, step):
    at = (zh * 4 + z + step) % 8
    return (x, at // 4, c, y, at % 4)


def along_plane(x, zh, c, y, z, step, first):
    if (c == 0) == first:
        return ((x + step) % 4, zh, c, y, z)
    return (x, zh, c, (y + step) % 4, z)


SWAP = permutation(lambda x, zh, c, y, z: (x, zh, 1 - c, y, z))
UP_Z = permutation(functools.partial(along_z, step=1))
DOWN_Z = permutation(functools.partial(along_z, step=-1))
UP_3Z = permutation(functools.partial(along_z, step=3))
DOWN_3Z = permutation(functools.partial(along_z, step=-3))
UP_FIRST = permutation(functools.partial(along_plane, step=1, first=True))
DOWN_FIRST = permutation(functools.partial(along_plane, step=-1, first=True))
UP_SECOND = permutation(functools.partial(along_plane, step=1, first=False))
DOWN_SECOND = permutation(functools.partial(along_plane, step=-1, first=False))


def dot(a, b):
    return lax.dot_general(a, b, (((1,), (0,)), ((), ())), preferred_element_type=F32)


def dot_t(a, b):
    return lax.dot_general(a, b, (((0,), (0,)), ((), ())), preferred_element_type=F32)


def normed(values):
    center = values - jnp.mean(values, axis=-1, keepdims=True)
    spread = jnp.mean(center * center, axis=-1, keepdims=True)
    return center * lax.rsqrt(spread + EPS)


def pool_kernel(
    fine_h, parent_h, medium_h, medium_parent_h, coarse_h, nbrs_h, weight_h,
    sender_out, pool_out, medium_out, slots_out, comp_out, member_out,
    fine, parent, medium, medium_parent, coarse, nbrs, weight, sems,
):
    pairs = (
        (parent_h, parent), (fine_h, fine), (medium_h, medium), (medium_parent_h, medium_parent),
        (coarse_h, coarse), (weight_h.at[pl.ds(0, D)], weight), (nbrs_h, nbrs),
    )
    copies = [pltpu.make_async_copy(source, target, sems.at[k]) for k, (source, target) in enumerate(pairs)]
    for copy in copies:
        copy.start()
    for copy in copies:
        copy.wait()
    member = (parent[...] == lax.broadcasted_iota(jnp.int32, (128, 1024), 0)).astype(F32)
    count = jnp.sum(member, axis=1, keepdims=True)
    member = member.astype(BF16)
    medium_pool = medium[...].astype(F32) + dot(member, fine[...]) / count
    medium_out[...] = medium_pool
    upper = (medium_parent[...] == lax.broadcasted_iota(jnp.int32, (16, 128), 0)).astype(F32)
    upper_count = jnp.sum(upper, axis=1, keepdims=True)
    total = jnp.dot(upper, medium_pool, precision=lax.Precision.HIGHEST, preferred_element_type=F32)
    pool = (coarse[...].astype(F32) + total / upper_count).astype(BF16)
    pool_out[...] = pool
    sender_out[...] = dot(pool, weight[...]).astype(BF16)
    upper = upper.astype(BF16)
    member_out[...] = jnp.concatenate([upper, upper], axis=0)
    comp = dot(upper, member).astype(BF16)
    comp_out[...] = jnp.concatenate([comp, comp], axis=0)
    here = {name: lax.axis_index(name) for name in AXES}
    row = nbrs[...] & 15
    owner = nbrs[...] >> 4
    z = owner & 3
    y = (owner >> 2) & 3
    c = (owner >> 4) & 1
    zh = (owner >> 5) & 1
    x = owner >> 6
    back = (here["zh"] * 4 + here["z"] - zh * 4 - z) & 7
    stream = c
    at = ((back + 1) & 7) * 16 + row
    step_x = (here["x"] - x) & 3
    step_y = (here["y"] - y) & 3
    order_x = jnp.where(step_x == 2, 3, jnp.where(step_x == 3, 2, step_x))
    order_y = jnp.where(step_y == 2, 3, jnp.where(step_y == 3, 2, step_y))
    at = at + jnp.where(stream == 0, order_x * 128 + order_y * 512, order_y * 128 + order_x * 512)
    slots_out[...] = at + jnp.where(stream == here["c"], 0, 2048)


def face_kernel(
    pool, fine_h, rows_h, counts, weight_h, edge_out_h, coarse_in_h, coarse_bias, nbrs_h,
    sender_out, centred_out, received_out, near_out, f0, f1, f2, f3, f4, f5,
    fine, rows, weight, edge_out, coarse_in, nbrs, sems,
):
    pairs = (
        (rows_h, rows), (fine_h, fine), (weight_h.at[pl.ds(0, D)], weight), (edge_out_h, edge_out),
        (coarse_in_h.at[pl.ds(D, D)], coarse_in), (nbrs_h, nbrs),
    )
    copies = [pltpu.make_async_copy(source, target, sems.at[k]) for k, (source, target) in enumerate(pairs)]
    for copy in copies:
        copy.start()
    for copy in copies:
        copy.wait()
    sender = dot(fine[...], weight[...]).astype(BF16)
    sender_out[...] = sender
    received_out[...] = dot(pool[...], coarse_in[...]) + coarse_bias[...]
    wide = edge_out[...].astype(F32)
    centred_out[...] = (wide - jnp.mean(wide, axis=1, keepdims=True)).astype(BF16)
    padded = jnp.concatenate([nbrs[...], jnp.zeros((2, 1024), jnp.int32)], axis=0)
    for block in range(8):
        near_out[block * 128 : (block + 1) * 128, :] = padded[:, block * 128 : (block + 1) * 128].T
    flat = jnp.concatenate(
        [rows[:, 128 * face : 128 * (face + 1)] for face in range(6)] + [jnp.zeros((2, 128), jnp.int32)], axis=0
    )
    columns = flat.T
    place = lax.broadcasted_iota(jnp.int32, (128, 1), 0)
    for face, face_out in enumerate((f0, f1, f2, f3, f4, f5)):
        wanted = jnp.where(place < counts[0, face], columns[:, face : face + 1], -1)
        picked = (wanted == lax.broadcasted_iota(jnp.int32, (128, 1024), 1)).astype(F32).astype(BF16)
        face_out[0] = dot(picked, sender).astype(BF16)


def table_kernel(sender, g0, g1, g2, g3, g4, g5, table_out, sems):
    copies = [pltpu.make_async_copy(sender, table_out.at[pl.ds(0, 1024)], sems.at[0])]
    for k, ghost in enumerate((g0, g1, g2, g3, g4, g5)):
        copies.append(
            pltpu.make_async_copy(ghost.at[0], table_out.at[pl.ds(1024 + 128 * k, 128)], sems.at[1 + k])
        )
    for copy in copies:
        copy.start()
    for copy in copies:
        copy.wait()


def edge_kernel(
    table, fine, nbrs, receive, bias, centred, gain, node_in, node_bias, node_out, node_gain,
    new_out,
    picked, hidden,
    *, first,
):
    def block_rows(block, lane):
        span = pl.ds(pl.multiple_of((first + block) * BLOCK, BLOCK), BLOCK)
        own = fine[span, :]
        near = nbrs[span, :]
        received = dot(own, receive[...]) + bias[...]
        for k in range(6):
            match = near[:, k : k + 1] == lax.broadcasted_iota(jnp.int32, (BLOCK, 1792), 1)
            picked[lane, k * BLOCK : (k + 1) * BLOCK, :] = match.astype(F32).astype(BF16)
        found = dot(picked[lane], table[...]).astype(BF16).astype(F32)
        hidden[lane] = jnp.maximum(found + jnp.concatenate([received] * 6, axis=0), 0.0).astype(BF16)
        out = dot(hidden[lane], centred[...])
        out = out * lax.rsqrt(jnp.mean(out * out, axis=-1, keepdims=True) + EPS)
        total = jnp.zeros((BLOCK, D), F32)
        for k in range(6):
            total = total + out[k * BLOCK : (k + 1) * BLOCK] * (near[:, k : k + 1] < 1792).astype(F32)
        incoming = (total * gain[...]).astype(BF16)
        both = jnp.concatenate([own, incoming], axis=1)
        node = jnp.maximum(dot(both, node_in[...]) + node_bias[...], 0.0).astype(BF16)
        here = pl.ds(pl.multiple_of(block * BLOCK, BLOCK), BLOCK)
        new_out[here, :] = own.astype(F32) + normed(dot(node, node_out[...])) * node_gain[...]

    def step(pair, carry):
        block_rows(pair * 2, 0)
        block_rows(pair * 2 + 1, 1)
        return carry

    lax.fori_loop(0, new_out.shape[0] // (2 * BLOCK), step, 0)


def columns_of(slots):
    places = slots[...]
    return jnp.concatenate([jnp.broadcast_to(places[:, k : k + 1], (16, 128)) for k in range(64)], axis=0)


def found_in(column, sources):
    lane = lax.broadcasted_iota(jnp.int32, (1024, 128), 1)
    total = jnp.zeros((1024, D), F32)
    for start, source in sources:
        picked = [
            (column == lane + (start + t * 128)).astype(F32).astype(BF16) for t in range(source.shape[0] // 128)
        ]
        total = total + dot(jnp.concatenate(picked, axis=1), source[...])
    return total


def gather_kernel(slots, m0, m1, m2, m3, m4, found_out):
    sources = ((0, m0), (512, m1), (1024, m2), (1536, m3), (1792, m4))
    found_out[...] = found_in(columns_of(slots), sources).astype(BF16)


def coarse_kernel(
    found, o0, o1, o2, o3, o4, slots, pool, medium, comp, member, *rest,
):
    *news, received, edge_out, edge_gain, node_in, node_bias, node_out, node_gain, fine_out, medium_out, coarse_out = rest
    pool_rows = pool[...]
    sources = ((2048, o0), (2560, o1), (3072, o2), (3584, o3), (3840, o4))
    total = found[...].astype(F32) + found_in(columns_of(slots), sources)
    hidden = jnp.maximum(total.reshape(64, 16, D) + received[...][None], 0.0).astype(BF16).reshape(1024, D)
    message = normed(dot(hidden, edge_out[...])) * edge_gain[...]
    incoming = jnp.sum(message.reshape(64, 16, D), axis=0).astype(BF16)
    both = jnp.concatenate([pool_rows, incoming], axis=1)
    hidden = jnp.maximum(dot(both, node_in[...]) + node_bias[...], 0.0).astype(BF16)
    delta = normed(dot(hidden, node_out[...])) * node_gain[...]
    coarse_out[...] = (pool_rows.astype(F32) + delta).astype(BF16)
    high = delta.astype(BF16)
    low = (delta - high.astype(F32)).astype(BF16)
    parts = jnp.concatenate([high, low], axis=0)
    medium_out[...] = (medium[...] + dot_t(member[...], parts)).astype(BF16)
    spread = dot_t(comp[...], parts)
    first = 0
    for new in news:
        last = first + new.shape[0]
        fine_out[first:last, :] = (new[...] + spread[first:last]).astype(BF16)
        first = last


def joined(*parts):
    return jnp.concatenate(parts, axis=0)


def sent(rows, pairs):
    return lax.ppermute(rows, AXES, pairs)


def local(
    fine_state, fine_nbrs, send_rows, ghost_counts, fine_parent, medium_state, medium_parent, coarse_state,
    coarse_nbrs, fine_edge_in, fine_edge_bias, fine_edge_out, fine_edge_gain, fine_node_in, fine_node_bias,
    fine_node_out, fine_node_gain, coarse_edge_in, coarse_edge_bias, coarse_edge_out, coarse_edge_gain,
    coarse_node_in, coarse_node_bias, coarse_node_out, coarse_node_gain,
):
    row = lambda vector: vector.reshape(1, -1)
    shaped = jax.ShapeDtypeStruct
    held = pl.BlockSpec(memory_space=pltpu.VMEM)
    far = pl.BlockSpec(memory_space=pltpu.HBM)
    scalars = pl.BlockSpec(memory_space=pltpu.SMEM)
    upper = pl.BlockSpec((D, D), lambda i: (1, 0), memory_space=pltpu.VMEM)
    tied = lax.optimization_barrier
    distant = functools.partial(pltpu.with_memory_space_constraint, memory_space=pltpu.HBM)

    def kernel(body, outs, specs, args, scratch=(), limit=32, cost=None):
        return pl.pallas_call(
            body,
            grid=(1,),
            out_shape=outs,
            in_specs=specs,
            out_specs=[held] * len(outs),
            scratch_shapes=list(scratch),
            compiler_params=pltpu.CompilerParams(vmem_limit_bytes=limit << 20),
            cost_estimate=cost,
        )(*args)

    sender, pool, medium_pool, slots, comp, member = kernel(
        pool_kernel,
        [
            shaped((16, D), BF16),
            shaped((16, D), BF16),
            shaped((128, D), F32),
            shaped((16, 64), jnp.int32),
            shaped((32, 1024), BF16),
            shaped((32, 128), BF16),
        ],
        [far] * 7,
        [
            distant(value)
            for value in (
                fine_state, row(fine_parent), medium_state, row(medium_parent), coarse_state, coarse_nbrs,
                coarse_edge_in,
            )
        ],
        [
            pltpu.VMEM((1024, D), BF16),
            pltpu.VMEM((1, 1024), jnp.int32),
            pltpu.VMEM((128, D), BF16),
            pltpu.VMEM((1, 128), jnp.int32),
            pltpu.VMEM((16, D), BF16),
            pltpu.VMEM((16, 64), jnp.int32),
            pltpu.VMEM((D, D), BF16),
            pltpu.SemaphoreType.DMA((7,)),
        ],
    )
    fine_sender, centred, received, near, *faces = kernel(
        face_kernel,
        [shaped((1024, D), BF16), shaped((D, D), BF16), shaped((16, D), F32), shaped((1024, 8), jnp.int32)]
        + [shaped((1, 128, D), BF16)] * 6,
        [held, far, far, scalars, far, far, far, held, far],
        (
            pool, distant(fine_state), distant(send_rows.reshape(1, 768)), ghost_counts, distant(fine_edge_in),
            distant(fine_edge_out), distant(coarse_edge_in), row(coarse_edge_bias),
            distant(fine_nbrs.T),
        ),
        [
            pltpu.VMEM((1024, D), BF16),
            pltpu.VMEM((1, 768), jnp.int32),
            pltpu.VMEM((D, D), BF16),
            pltpu.VMEM((D, D), BF16),
            pltpu.VMEM((D, D), BF16),
            pltpu.VMEM((6, 1024), jnp.int32),
            pltpu.SemaphoreType.DMA((6,)),
        ],
    )

    def faced(face):
        axes = (("x", "zh", "c"), "y")[face // 2]
        count = lax.axis_size(axes)
        pairs = [(k, k + 1) for k in range(count - 1)]
        return lax.ppermute(faces[face], axes, [(b, a) for a, b in pairs] if face % 2 == 0 else pairs)

    low, high = sent(sender, UP_Z), sent(sender, DOWN_Z)
    low, high, faces[0], faces[1] = tied((low, high, faces[0], faces[1]))
    three = joined(high, sender, low)
    lower, higher = sent(three, UP_3Z), sent(three[16:], DOWN_3Z)
    low_x, high_x = faced(1), faced(0)
    lower, higher, *faces[2:] = tied((lower, higher, *faces[2:]))
    column = joined(three, lower, higher)
    up, down = sent(column, UP_FIRST), sent(column, DOWN_FIRST)
    low_y, high_y = faced(3), faced(2)
    low_z, high_z = sent(faces[5], UP_Z), sent(faces[4], DOWN_Z)
    near_faces = [low_x, high_x, low_y, high_y, low_z, high_z]
    (table,) = kernel(
        table_kernel,
        [shaped((1792, D), BF16)],
        [pl.BlockSpec(memory_space=pl.ANY)] * 7,
        (fine_sender, *near_faces),
        [pltpu.SemaphoreType.DMA((7,))],
    )
    news = []

    def edges(blocks):
        first = sum(new.shape[0] for new in news) // BLOCK
        news.extend(
            kernel(
                functools.partial(edge_kernel, first=first),
                [shaped((blocks * BLOCK, D), F32)],
                [held] * 3 + [upper] + [held] * 7,
                (
                    table, fine_state, near, fine_edge_in, row(fine_edge_bias), centred, row(fine_edge_gain),
                    fine_node_in, row(fine_node_bias), fine_node_out, row(fine_node_gain),
                ),
                [pltpu.VMEM((2, 6 * BLOCK, 1792), BF16), pltpu.VMEM((2, 6 * BLOCK, D), BF16)],
                cost=pl.CostEstimate(
                    flops=blocks * 1_700_000_000, bytes_accessed=blocks * 3_000_000, transcendentals=0
                ),
            )
        )

    rest = [sent(up[:64], UP_FIRST), sent(down[64:], DOWN_FIRST)]
    line = joined(column, up, down, *rest)
    table, line = tied((table, line))
    up, down = sent(line, UP_SECOND), sent(line, DOWN_SECOND)
    edges(SHARES[0])
    up, down, news[-1] = tied((up, down, news[-1]))
    table, up = tied((table, up))
    rest = [sent(up[:256], UP_SECOND), sent(down[256:], DOWN_SECOND)]
    edges(SHARES[1])
    line, up, down, *rest, news[-1] = tied((line, up, down, *rest, news[-1]))
    table, rest[0] = tied((table, rest[0]))
    others = [sent(part, SWAP) for part in (line, up, down, *rest)]
    edges(SHARES[2])
    (found,) = kernel(
        gather_kernel, [shaped((1024, D), BF16)], [held] * 6, (slots, line, up, down, *rest), limit=40,
        cost=pl.CostEstimate(flops=2_000_000_000, bytes_accessed=4_000_000, transcendentals=0),
    )
    fine_out, medium_out, coarse_out = kernel(
        coarse_kernel,
        [shaped((1024, D), BF16), shaped((128, D), BF16), shaped((16, D), BF16)],
        [held] * (18 + len(news)),
        (
            found, *others, slots, pool, medium_pool, comp, member, *news, received,
            coarse_edge_out, row(coarse_edge_gain), coarse_node_in, row(coarse_node_bias), coarse_node_out,
            row(coarse_node_gain),
        ),
        limit=48,
    )
    return fine_out, medium_out, coarse_out


def solution(mesh):
    torus = Mesh(mesh.devices.reshape(SIZES), AXES)
    rows = P(AXES, None)
    placed = (rows, rows, P(AXES, None, None), rows, P(AXES), rows, P(AXES), rows, rows) + (P(),) * 16
    return jax.shard_map(local, mesh=torus, in_specs=placed, out_specs=(rows, rows, rows), check_vma=False)
```

```python
import functools
import itertools

import jax
import jax.numpy as jnp
from jax import lax
from jax.experimental import pallas as pl
from jax.experimental.pallas import tpu as pltpu
from jax.sharding import Mesh
from jax.sharding import PartitionSpec as P

AXES = ("x", "zh", "c", "y", "z")
SIZES = (4, 2, 2, 4, 4)
EPS = 1e-05
F32 = jnp.float32
BF16 = jnp.bfloat16
D = 512
BLOCK = 128
SHARES = (4, 2, 2)


def linear(place):
    number = 0
    for size, at in zip(SIZES, place):
        number = number * size + at
    return number


def permutation(move):
    pairs = []
    for place in itertools.product(*(range(size) for size in SIZES)):
        target = move(*place)
        if target is not None:
            pairs.append((linear(place), linear(target)))
    return pairs


def along_z(x, zh, c, y, z, step):
    at = (zh * 4 + z + step) % 8
    return (x, at // 4, c, y, at % 4)


def along_plane(x, zh, c, y, z, step, first):
    if (c == 0) == first:
        return ((x + step) % 4, zh, c, y, z)
    return (x, zh, c, (y + step) % 4, z)


SWAP = permutation(lambda x, zh, c, y, z: (x, zh, 1 - c, y, z))
UP_Z = permutation(functools.partial(along_z, step=1))
DOWN_Z = permutation(functools.partial(along_z, step=-1))
UP_3Z = permutation(functools.partial(along_z, step=3))
DOWN_3Z = permutation(functools.partial(along_z, step=-3))
UP_FIRST = permutation(functools.partial(along_plane, step=1, first=True))
DOWN_FIRST = permutation(functools.partial(along_plane, step=-1, first=True))
UP_SECOND = permutation(functools.partial(along_plane, step=1, first=False))
DOWN_SECOND = permutation(functools.partial(along_plane, step=-1, first=False))


def dot(a, b):
    return lax.dot_general(a, b, (((1,), (0,)), ((), ())), preferred_element_type=F32)


def dot_t(a, b):
    return lax.dot_general(a, b, (((0,), (0,)), ((), ())), preferred_element_type=F32)


def normed(values):
    center = values - jnp.mean(values, axis=-1, keepdims=True)
    spread = jnp.mean(center * center, axis=-1, keepdims=True)
    return center * lax.rsqrt(spread + EPS)


def first_kernel(
    fine_h, parent_h, medium_h, medium_parent_h, coarse_h, nbrs_h, weight_h,
    rows_h, counts_h, fine_in_h, edge_out_h, coarse_bias_h, fine_near_h,
    sender_out, pool_out, medium_out, slots_out, comp_out, member_out,
    fine_sender_out, centred_out, received_out, near_out, f0, f1, f2, f3, f4, f5,
    fine, parent, medium, medium_parent, coarse, nbrs, weight, rows, fine_in, edge_out, coarse_in, fine_near,
    counts, coarse_bias, sems,
):
    pairs = (
        (parent_h, parent), (fine_h, fine), (medium_h, medium), (medium_parent_h, medium_parent),
        (coarse_h, coarse), (weight_h.at[pl.ds(0, D)], weight), (nbrs_h, nbrs), (rows_h, rows),
        (fine_in_h.at[pl.ds(0, D)], fine_in), (edge_out_h, edge_out), (weight_h.at[pl.ds(D, D)], coarse_in),
        (fine_near_h, fine_near), (counts_h, counts), (coarse_bias_h, coarse_bias),
    )
    copies = [pltpu.make_async_copy(source, target, sems.at[k]) for k, (source, target) in enumerate(pairs)]
    for copy in copies:
        copy.start()
    for copy in copies[:7]:
        copy.wait()
    member = (parent[...] == lax.broadcasted_iota(jnp.int32, (128, 1024), 0)).astype(F32)
    count = jnp.sum(member, axis=1, keepdims=True)
    member = member.astype(BF16)
    medium_pool = medium[...].astype(F32) + dot(member, fine[...]) / count
    medium_out[...] = medium_pool
    upper = (medium_parent[...] == lax.broadcasted_iota(jnp.int32, (16, 128), 0)).astype(F32)
    upper_count = jnp.sum(upper, axis=1, keepdims=True)
    total = jnp.dot(upper, medium_pool, precision=lax.Precision.HIGHEST, preferred_element_type=F32)
    pool = (coarse[...].astype(F32) + total / upper_count).astype(BF16)
    pool_out[...] = pool
    sender_out[...] = dot(pool, weight[...]).astype(BF16)
    upper = upper.astype(BF16)
    member_out[...] = jnp.concatenate([upper, upper], axis=0)
    comp = dot(upper, member).astype(BF16)
    comp_out[...] = jnp.concatenate([comp, comp], axis=0)
    here = {name: lax.axis_index(name) for name in AXES}
    row = nbrs[...] & 15
    owner = nbrs[...] >> 4
    z = owner & 3
    y = (owner >> 2) & 3
    c = (owner >> 4) & 1
    zh = (owner >> 5) & 1
    x = owner >> 6
    back = (here["zh"] * 4 + here["z"] - zh * 4 - z) & 7
    stream = c
    at = ((back + 1) & 7) * 16 + row
    step_x = (here["x"] - x) & 3
    step_y = (here["y"] - y) & 3
    order_x = jnp.where(step_x == 2, 3, jnp.where(step_x == 3, 2, step_x))
    order_y = jnp.where(step_y == 2, 3, jnp.where(step_y == 3, 2, step_y))
    at = at + jnp.where(stream == 0, order_x * 128 + order_y * 512, order_y * 128 + order_x * 512)
    slots_out[...] = at + jnp.where(stream == here["c"], 0, 2048)
    for copy in copies[7:]:
        copy.wait()
    fine_sender = dot(fine[...], fine_in[...]).astype(BF16)
    fine_sender_out[...] = fine_sender
    received_out[...] = dot(pool, coarse_in[...]) + coarse_bias[...]
    wide = edge_out[...].astype(F32)
    centred_out[...] = (wide - jnp.mean(wide, axis=1, keepdims=True)).astype(BF16)
    padded = jnp.concatenate([fine_near[...], jnp.zeros((2, 1024), jnp.int32)], axis=0)
    for block in range(8):
        near_out[block * 128 : (block + 1) * 128, :] = padded[:, block * 128 : (block + 1) * 128].T
    flat = jnp.concatenate(
        [rows[:, 128 * face : 128 * (face + 1)] for face in range(6)] + [jnp.zeros((2, 128), jnp.int32)], axis=0
    )
    columns = flat.T
    place = lax.broadcasted_iota(jnp.int32, (128, 1), 0)
    for face, face_out in enumerate((f0, f1, f2, f3, f4, f5)):
        wanted = jnp.where(place < counts[0, face], columns[:, face : face + 1], -1)
        picked = (wanted == lax.broadcasted_iota(jnp.int32, (128, 1024), 1)).astype(F32).astype(BF16)
        face_out[0] = dot(picked, fine_sender).astype(BF16)


def table_kernel(sender, g0, g1, g2, g3, g4, g5, table_out, sems):
    copies = [pltpu.make_async_copy(sender, table_out.at[pl.ds(0, 1024)], sems.at[0])]
    for k, ghost in enumerate((g0, g1, g2, g3, g4, g5)):
        copies.append(
            pltpu.make_async_copy(ghost.at[0], table_out.at[pl.ds(1024 + 128 * k, 128)], sems.at[1 + k])
        )
    for copy in copies:
        copy.start()
    for copy in copies:
        copy.wait()


def edge_kernel(
    table, fine, nbrs, receive, bias, centred, gain, node_in, node_bias, node_out, node_gain,
    new_out,
    picked, hidden,
    *, first,
):
    def block_rows(block, lane):
        span = pl.ds(pl.multiple_of((first + block) * BLOCK, BLOCK), BLOCK)
        own = fine[span, :]
        near = nbrs[span, :]
        received = dot(own, receive[...]) + bias[...]
        for k in range(6):
            match = near[:, k : k + 1] == lax.broadcasted_iota(jnp.int32, (BLOCK, 1792), 1)
            picked[lane, k * BLOCK : (k + 1) * BLOCK, :] = match.astype(F32).astype(BF16)
        found = dot(picked[lane], table[...]).astype(BF16).astype(F32)
        hidden[lane] = jnp.maximum(found + jnp.concatenate([received] * 6, axis=0), 0.0).astype(BF16)
        out = dot(hidden[lane], centred[...])
        out = out * lax.rsqrt(jnp.mean(out * out, axis=-1, keepdims=True) + EPS)
        total = jnp.zeros((BLOCK, D), F32)
        for k in range(6):
            total = total + out[k * BLOCK : (k + 1) * BLOCK] * (near[:, k : k + 1] < 1792).astype(F32)
        incoming = (total * gain[...]).astype(BF16)
        both = jnp.concatenate([own, incoming], axis=1)
        node = jnp.maximum(dot(both, node_in[...]) + node_bias[...], 0.0).astype(BF16)
        here = pl.ds(pl.multiple_of(block * BLOCK, BLOCK), BLOCK)
        new_out[here, :] = own.astype(F32) + normed(dot(node, node_out[...])) * node_gain[...]

    def step(pair, carry):
        block_rows(pair * 2, 0)
        block_rows(pair * 2 + 1, 1)
        return carry

    lax.fori_loop(0, new_out.shape[0] // (2 * BLOCK), step, 0)


def columns_of(slots):
    places = slots[...]
    return jnp.concatenate([jnp.broadcast_to(places[:, k : k + 1], (16, 128)) for k in range(64)], axis=0)


def found_in(column, sources):
    lane = lax.broadcasted_iota(jnp.int32, (1024, 128), 1)
    total = jnp.zeros((1024, D), F32)
    for start, source in sources:
        picked = [
            (column == lane + (start + t * 128)).astype(F32).astype(BF16) for t in range(source.shape[0] // 128)
        ]
        total = total + dot(jnp.concatenate(picked, axis=1), source[...])
    return total


def gather_kernel(slots, m0, m1, m2, m3, m4, found_out):
    sources = ((0, m0), (512, m1), (1024, m2), (1536, m3), (1792, m4))
    found_out[...] = found_in(columns_of(slots), sources).astype(BF16)


def coarse_kernel(
    found, o0, o1, o2, o3, o4, slots, pool, medium, comp, member, *rest,
):
    *news, received, edge_out, edge_gain, node_in, node_bias, node_out, node_gain, fine_out, medium_out, coarse_out = rest
    pool_rows = pool[...]
    sources = ((2048, o0), (2560, o1), (3072, o2), (3584, o3), (3840, o4))
    total = found[...].astype(F32) + found_in(columns_of(slots), sources)
    hidden = jnp.maximum(total.reshape(64, 16, D) + received[...][None], 0.0).astype(BF16).reshape(1024, D)
    message = normed(dot(hidden, edge_out[...])) * edge_gain[...]
    incoming = jnp.sum(message.reshape(64, 16, D), axis=0).astype(BF16)
    both = jnp.concatenate([pool_rows, incoming], axis=1)
    hidden = jnp.maximum(dot(both, node_in[...]) + node_bias[...], 0.0).astype(BF16)
    delta = normed(dot(hidden, node_out[...])) * node_gain[...]
    coarse_out[...] = (pool_rows.astype(F32) + delta).astype(BF16)
    high = delta.astype(BF16)
    low = (delta - high.astype(F32)).astype(BF16)
    parts = jnp.concatenate([high, low], axis=0)
    medium_out[...] = (medium[...] + dot_t(member[...], parts)).astype(BF16)
    spread = dot_t(comp[...], parts)
    first = 0
    for new in news:
        last = first + new.shape[0]
        fine_out[first:last, :] = (new[...] + spread[first:last]).astype(BF16)
        first = last


def joined(*parts):
    return jnp.concatenate(parts, axis=0)


def sent(rows, pairs):
    return lax.ppermute(rows, AXES, pairs)


def local(
    fine_state, fine_nbrs, send_rows, ghost_counts, fine_parent, medium_state, medium_parent, coarse_state,
    coarse_nbrs, fine_edge_in, fine_edge_bias, fine_edge_out, fine_edge_gain, fine_node_in, fine_node_bias,
    fine_node_out, fine_node_gain, coarse_edge_in, coarse_edge_bias, coarse_edge_out, coarse_edge_gain,
    coarse_node_in, coarse_node_bias, coarse_node_out, coarse_node_gain,
):
    row = lambda vector: vector.reshape(1, -1)
    shaped = jax.ShapeDtypeStruct
    held = pl.BlockSpec(memory_space=pltpu.VMEM)
    far = pl.BlockSpec(memory_space=pltpu.HBM)
    upper = pl.BlockSpec((D, D), lambda i: (1, 0), memory_space=pltpu.VMEM)
    tied = lax.optimization_barrier
    distant = functools.partial(pltpu.with_memory_space_constraint, memory_space=pltpu.HBM)

    def kernel(body, outs, specs, args, scratch=(), limit=32, cost=None):
        return pl.pallas_call(
            body,
            grid=(1,),
            out_shape=outs,
            in_specs=specs,
            out_specs=[held] * len(outs),
            scratch_shapes=list(scratch),
            compiler_params=pltpu.CompilerParams(vmem_limit_bytes=limit << 20),
            cost_estimate=cost,
        )(*args)

    sender, pool, medium_pool, slots, comp, member, fine_sender, centred, received, near, *faces = kernel(
        first_kernel,
        [
            shaped((16, D), BF16),
            shaped((16, D), BF16),
            shaped((128, D), F32),
            shaped((16, 64), jnp.int32),
            shaped((32, 1024), BF16),
            shaped((32, 128), BF16),
            shaped((1024, D), BF16),
            shaped((D, D), BF16),
            shaped((16, D), F32),
            shaped((1024, 8), jnp.int32),
        ]
        + [shaped((1, 128, D), BF16)] * 6,
        [far] * 13,
        (
            distant(fine_state), distant(row(fine_parent)), distant(medium_state), distant(row(medium_parent)),
            distant(coarse_state), distant(coarse_nbrs), distant(coarse_edge_in), distant(send_rows.reshape(1, 768)),
            distant(ghost_counts), distant(fine_edge_in), distant(fine_edge_out), distant(row(coarse_edge_bias)),
            distant(fine_nbrs.T),
        ),
        [
            pltpu.VMEM((1024, D), BF16),
            pltpu.VMEM((1, 1024), jnp.int32),
            pltpu.VMEM((128, D), BF16),
            pltpu.VMEM((1, 128), jnp.int32),
            pltpu.VMEM((16, D), BF16),
            pltpu.VMEM((16, 64), jnp.int32),
            pltpu.VMEM((D, D), BF16),
            pltpu.VMEM((1, 768), jnp.int32),
            pltpu.VMEM((D, D), BF16),
            pltpu.VMEM((D, D), BF16),
            pltpu.VMEM((D, D), BF16),
            pltpu.VMEM((6, 1024), jnp.int32),
            pltpu.SMEM((1, 6), jnp.int32),
            pltpu.VMEM((1, D), F32),
            pltpu.SemaphoreType.DMA((14,)),
        ],
    )

    def faced(face):
        axes = (("x", "zh", "c"), "y")[face // 2]
        count = lax.axis_size(axes)
        pairs = [(k, k + 1) for k in range(count - 1)]
        return lax.ppermute(faces[face], axes, [(b, a) for a, b in pairs] if face % 2 == 0 else pairs)

    low, high = sent(sender, UP_Z), sent(sender, DOWN_Z)
    low_x = faced(1)
    low, high, faces[0] = tied((low, high, faces[0]))
    three = joined(high, sender, low)
    lower, higher = sent(three, UP_3Z), sent(three[16:], DOWN_3Z)
    high_x = faced(0)
    lower, higher, *faces[2:] = tied((lower, higher, *faces[2:]))
    column = joined(three, lower, higher)
    up, down = sent(column, UP_FIRST), sent(column, DOWN_FIRST)
    low_y, high_y = faced(3), faced(2)
    low_z, high_z = sent(faces[5], UP_Z), sent(faces[4], DOWN_Z)
    near_faces = [low_x, high_x, low_y, high_y, low_z, high_z]
    (table,) = kernel(
        table_kernel,
        [shaped((1792, D), BF16)],
        [pl.BlockSpec(memory_space=pl.ANY)] * 7,
        (fine_sender, *near_faces),
        [pltpu.SemaphoreType.DMA((7,))],
    )
    news = []

    def edges(blocks):
        first = sum(new.shape[0] for new in news) // BLOCK
        news.extend(
            kernel(
                functools.partial(edge_kernel, first=first),
                [shaped((blocks * BLOCK, D), F32)],
                [held] * 3 + [upper] + [held] * 7,
                (
                    table, fine_state, near, fine_edge_in, row(fine_edge_bias), centred, row(fine_edge_gain),
                    fine_node_in, row(fine_node_bias), fine_node_out, row(fine_node_gain),
                ),
                [pltpu.VMEM((2, 6 * BLOCK, 1792), BF16), pltpu.VMEM((2, 6 * BLOCK, D), BF16)],
                cost=pl.CostEstimate(
                    flops=blocks * 1_700_000_000, bytes_accessed=blocks * 3_000_000, transcendentals=0
                ),
            )
        )

    rest = [sent(up[:64], UP_FIRST), sent(down[64:], DOWN_FIRST)]
    line = joined(column, up, down, *rest)
    table, line = tied((table, line))
    up, down = sent(line, UP_SECOND), sent(line, DOWN_SECOND)
    edges(SHARES[0])
    up, down, news[-1] = tied((up, down, news[-1]))
    table, up = tied((table, up))
    rest = [sent(up[:256], UP_SECOND), sent(down[256:], DOWN_SECOND)]
    edges(SHARES[1])
    line, up, down, *rest, news[-1] = tied((line, up, down, *rest, news[-1]))
    table, rest[0] = tied((table, rest[0]))
    others = [sent(part, SWAP) for part in (line, up, down, *rest)]
    edges(SHARES[2])
    (found,) = kernel(
        gather_kernel, [shaped((1024, D), BF16)], [held] * 6, (slots, line, up, down, *rest), limit=40,
        cost=pl.CostEstimate(flops=2_000_000_000, bytes_accessed=4_000_000, transcendentals=0),
    )
    fine_out, medium_out, coarse_out = kernel(
        coarse_kernel,
        [shaped((1024, D), BF16), shaped((128, D), BF16), shaped((16, D), BF16)],
        [held] * (18 + len(news)),
        (
            found, *others, slots, pool, medium_pool, comp, member, *news, received,
            coarse_edge_out, row(coarse_edge_gain), coarse_node_in, row(coarse_node_bias), coarse_node_out,
            row(coarse_node_gain),
        ),
        limit=48,
    )
    return fine_out, medium_out, coarse_out


def solution(mesh):
    torus = Mesh(mesh.devices.reshape(SIZES), AXES)
    rows = P(AXES, None)
    placed = (rows, rows, P(AXES, None, None), rows, P(AXES), rows, P(AXES), rows, rows) + (P(),) * 16
    return jax.shard_map(local, mesh=torus, in_specs=placed, out_specs=(rows, rows, rows), check_vma=False)
```

```python
import functools
import itertools

import jax
import jax.numpy as jnp
from jax import lax
from jax.experimental import pallas as pl
from jax.experimental.pallas import tpu as pltpu
from jax.sharding import Mesh
from jax.sharding import PartitionSpec as P

AXES = ("x", "zh", "c", "y", "z")
SIZES = (4, 2, 2, 4, 4)
EPS = 1e-05
F32 = jnp.float32
BF16 = jnp.bfloat16
D = 512
BLOCK = 128
SHARES = (4, 2, 2)


def linear(place):
    number = 0
    for size, at in zip(SIZES, place):
        number = number * size + at
    return number


def permutation(move):
    pairs = []
    for place in itertools.product(*(range(size) for size in SIZES)):
        target = move(*place)
        if target is not None:
            pairs.append((linear(place), linear(target)))
    return pairs


def along_z(x, zh, c, y, z, step):
    at = (zh * 4 + z + step) % 8
    return (x, at // 4, c, y, at % 4)


def along_plane(x, zh, c, y, z, step, first):
    if (c == 0) == first:
        return ((x + step) % 4, zh, c, y, z)
    return (x, zh, c, (y + step) % 4, z)


SWAP = permutation(lambda x, zh, c, y, z: (x, zh, 1 - c, y, z))
UP_Z = permutation(functools.partial(along_z, step=1))
DOWN_Z = permutation(functools.partial(along_z, step=-1))
UP_3Z = permutation(functools.partial(along_z, step=3))
DOWN_3Z = permutation(functools.partial(along_z, step=-3))
UP_FIRST = permutation(functools.partial(along_plane, step=1, first=True))
DOWN_FIRST = permutation(functools.partial(along_plane, step=-1, first=True))
UP_SECOND = permutation(functools.partial(along_plane, step=1, first=False))
DOWN_SECOND = permutation(functools.partial(along_plane, step=-1, first=False))


def dot(a, b):
    return lax.dot_general(a, b, (((1,), (0,)), ((), ())), preferred_element_type=F32)


def dot_t(a, b):
    return lax.dot_general(a, b, (((0,), (0,)), ((), ())), preferred_element_type=F32)


def normed(values):
    center = values - jnp.mean(values, axis=-1, keepdims=True)
    spread = jnp.mean(center * center, axis=-1, keepdims=True)
    return center * lax.rsqrt(spread + EPS)


def first_kernel(
    fine_h, parent_h, medium_h, medium_parent_h, coarse_h, nbrs_h, weight_h,
    rows_h, counts_h, fine_in_h, edge_out_h, coarse_bias_h, fine_near_h,
    sender_out, pool_out, medium_out, slots_out, comp_out, member_out,
    fine_sender_out, centred_out, received_out, near_out, f0, f1, f2, f3, f4, f5,
    fine, parent, medium, medium_parent, coarse, nbrs, weight, rows, fine_in, edge_out, coarse_in, fine_near,
    counts, coarse_bias, sems,
):
    pairs = (
        (parent_h, parent), (fine_h, fine), (medium_h, medium), (medium_parent_h, medium_parent),
        (coarse_h, coarse), (weight_h.at[pl.ds(0, D)], weight), (nbrs_h, nbrs), (rows_h, rows),
        (fine_in_h.at[pl.ds(0, D)], fine_in), (edge_out_h, edge_out), (weight_h.at[pl.ds(D, D)], coarse_in),
        (fine_near_h, fine_near), (counts_h, counts), (coarse_bias_h, coarse_bias),
    )
    copies = [pltpu.make_async_copy(source, target, sems.at[k]) for k, (source, target) in enumerate(pairs)]
    for copy in copies:
        copy.start()
    for copy in copies[:7]:
        copy.wait()
    member = (parent[...] == lax.broadcasted_iota(jnp.int32, (128, 1024), 0)).astype(F32)
    count = jnp.sum(member, axis=1, keepdims=True)
    member = member.astype(BF16)
    medium_pool = medium[...].astype(F32) + dot(member, fine[...]) / count
    medium_out[...] = medium_pool
    upper = (medium_parent[...] == lax.broadcasted_iota(jnp.int32, (16, 128), 0)).astype(F32)
    upper_count = jnp.sum(upper, axis=1, keepdims=True)
    total = jnp.dot(upper, medium_pool, precision=lax.Precision.HIGHEST, preferred_element_type=F32)
    pool = (coarse[...].astype(F32) + total / upper_count).astype(BF16)
    pool_out[...] = pool
    sender_out[...] = dot(pool, weight[...]).astype(BF16)
    upper = upper.astype(BF16)
    member_out[...] = jnp.concatenate([upper, upper], axis=0)
    comp = dot(upper, member).astype(BF16)
    comp_out[...] = jnp.concatenate([comp, comp], axis=0)
    here = {name: lax.axis_index(name) for name in AXES}
    row = nbrs[...] & 15
    owner = nbrs[...] >> 4
    z = owner & 3
    y = (owner >> 2) & 3
    c = (owner >> 4) & 1
    zh = (owner >> 5) & 1
    x = owner >> 6
    back = (here["zh"] * 4 + here["z"] - zh * 4 - z) & 7
    stream = c
    at = ((back + 1) & 7) * 16 + row
    step_x = (here["x"] - x) & 3
    step_y = (here["y"] - y) & 3
    order_x = jnp.where(step_x == 2, 3, jnp.where(step_x == 3, 2, step_x))
    order_y = jnp.where(step_y == 2, 3, jnp.where(step_y == 3, 2, step_y))
    at = at + jnp.where(stream == 0, order_x * 128 + order_y * 512, order_y * 128 + order_x * 512)
    slots_out[...] = at + jnp.where(stream == here["c"], 0, 2048)
    for copy in copies[7:]:
        copy.wait()
    fine_sender = dot(fine[...], fine_in[...]).astype(BF16)
    fine_sender_out[...] = fine_sender
    received_out[...] = dot(pool, coarse_in[...]) + coarse_bias[...]
    wide = edge_out[...].astype(F32)
    centred_out[...] = (wide - jnp.mean(wide, axis=1, keepdims=True)).astype(BF16)
    padded = jnp.concatenate([fine_near[...], jnp.zeros((2, 1024), jnp.int32)], axis=0)
    for block in range(8):
        near_out[block * 128 : (block + 1) * 128, :] = padded[:, block * 128 : (block + 1) * 128].T
    flat = jnp.concatenate(
        [rows[:, 128 * face : 128 * (face + 1)] for face in range(6)] + [jnp.zeros((2, 128), jnp.int32)], axis=0
    )
    columns = flat.T
    place = lax.broadcasted_iota(jnp.int32, (128, 1), 0)
    for face, face_out in enumerate((f0, f1, f2, f3, f4, f5)):
        wanted = jnp.where(place < counts[0, face], columns[:, face : face + 1], -1)
        picked = (wanted == lax.broadcasted_iota(jnp.int32, (128, 1024), 1)).astype(F32).astype(BF16)
        face_out[0] = dot(picked, fine_sender).astype(BF16)


def table_kernel(sender, g0, g1, g2, g3, g4, g5, table_out, sems):
    copies = [pltpu.make_async_copy(sender, table_out.at[pl.ds(0, 1024)], sems.at[0])]
    for k, ghost in enumerate((g0, g1, g2, g3, g4, g5)):
        copies.append(
            pltpu.make_async_copy(ghost.at[0], table_out.at[pl.ds(1024 + 128 * k, 128)], sems.at[1 + k])
        )
    for copy in copies:
        copy.start()
    for copy in copies:
        copy.wait()


def edge_kernel(
    table, fine, nbrs, receive, bias, centred, gain, node_in, node_bias, node_out, node_gain,
    new_out,
    picked, hidden,
    *, first,
):
    def block_rows(block, lane):
        span = pl.ds(pl.multiple_of((first + block) * BLOCK, BLOCK), BLOCK)
        own = fine[span, :]
        near = nbrs[span, :]
        received = dot(own, receive[...]) + bias[...]
        for k in range(6):
            match = near[:, k : k + 1] == lax.broadcasted_iota(jnp.int32, (BLOCK, 1792), 1)
            picked[lane, k * BLOCK : (k + 1) * BLOCK, :] = match.astype(F32).astype(BF16)
        found = dot(picked[lane], table[...]).astype(BF16).astype(F32)
        hidden[lane] = jnp.maximum(found + jnp.concatenate([received] * 6, axis=0), 0.0).astype(BF16)
        out = dot(hidden[lane], centred[...])
        out = out * lax.rsqrt(jnp.mean(out * out, axis=-1, keepdims=True) + EPS)
        total = jnp.zeros((BLOCK, D), F32)
        for k in range(6):
            total = total + out[k * BLOCK : (k + 1) * BLOCK] * (near[:, k : k + 1] < 1792).astype(F32)
        incoming = (total * gain[...]).astype(BF16)
        both = jnp.concatenate([own, incoming], axis=1)
        node = jnp.maximum(dot(both, node_in[...]) + node_bias[...], 0.0).astype(BF16)
        here = pl.ds(pl.multiple_of(block * BLOCK, BLOCK), BLOCK)
        new_out[here, :] = own.astype(F32) + normed(dot(node, node_out[...])) * node_gain[...]

    def step(pair, carry):
        block_rows(pair * 2, 0)
        block_rows(pair * 2 + 1, 1)
        return carry

    lax.fori_loop(0, new_out.shape[0] // (2 * BLOCK), step, 0)


def columns_of(slots):
    places = slots[...]
    return jnp.concatenate([jnp.broadcast_to(places[:, k : k + 1], (16, 128)) for k in range(64)], axis=0)


def found_in(column, sources):
    lane = lax.broadcasted_iota(jnp.int32, (1024, 128), 1)
    total = jnp.zeros((1024, D), F32)
    for start, source in sources:
        picked = [
            (column == lane + (start + t * 128)).astype(F32).astype(BF16) for t in range(source.shape[0] // 128)
        ]
        total = total + dot(jnp.concatenate(picked, axis=1), source[...])
    return total


def gather_kernel(slots, m0, m1, m2, m3, m4, found_out):
    sources = ((0, m0), (512, m1), (1024, m2), (1536, m3), (1792, m4))
    found_out[...] = found_in(columns_of(slots), sources).astype(BF16)


def coarse_kernel(
    found, o0, o1, o2, o3, o4, slots, pool, medium, comp, member, *rest,
):
    *news, received, edge_out, edge_gain, node_in, node_bias, node_out, node_gain, fine_out, medium_out, coarse_out = rest
    pool_rows = pool[...]
    sources = ((2048, o0), (2560, o1), (3072, o2), (3584, o3), (3840, o4))
    total = found[...].astype(F32) + found_in(columns_of(slots), sources)
    hidden = jnp.maximum(total.reshape(64, 16, D) + received[...][None], 0.0).astype(BF16).reshape(1024, D)
    message = normed(dot(hidden, edge_out[...])) * edge_gain[...]
    incoming = jnp.sum(message.reshape(64, 16, D), axis=0).astype(BF16)
    both = jnp.concatenate([pool_rows, incoming], axis=1)
    hidden = jnp.maximum(dot(both, node_in[...]) + node_bias[...], 0.0).astype(BF16)
    delta = normed(dot(hidden, node_out[...])) * node_gain[...]
    coarse_out[...] = (pool_rows.astype(F32) + delta).astype(BF16)
    high = delta.astype(BF16)
    low = (delta - high.astype(F32)).astype(BF16)
    parts = jnp.concatenate([high, low], axis=0)
    medium_out[...] = (medium[...] + dot_t(member[...], parts)).astype(BF16)
    spread = dot_t(comp[...], parts)
    first = 0
    for new in news:
        last = first + new.shape[0]
        fine_out[first:last, :] = (new[...] + spread[first:last]).astype(BF16)
        first = last


def joined(*parts):
    return jnp.concatenate(parts, axis=0)


def sent(rows, pairs):
    return lax.ppermute(rows, AXES, pairs)


def local(
    fine_state, fine_nbrs, send_rows, ghost_counts, fine_parent, medium_state, medium_parent, coarse_state,
    coarse_nbrs, fine_edge_in, fine_edge_bias, fine_edge_out, fine_edge_gain, fine_node_in, fine_node_bias,
    fine_node_out, fine_node_gain, coarse_edge_in, coarse_edge_bias, coarse_edge_out, coarse_edge_gain,
    coarse_node_in, coarse_node_bias, coarse_node_out, coarse_node_gain,
):
    row = lambda vector: vector.reshape(1, -1)
    shaped = jax.ShapeDtypeStruct
    held = pl.BlockSpec(memory_space=pltpu.VMEM)
    far = pl.BlockSpec(memory_space=pltpu.HBM)
    upper = pl.BlockSpec((D, D), lambda i: (1, 0), memory_space=pltpu.VMEM)
    tied = lax.optimization_barrier
    distant = functools.partial(pltpu.with_memory_space_constraint, memory_space=pltpu.HBM)

    def kernel(body, outs, specs, args, scratch=(), limit=32, cost=None):
        return pl.pallas_call(
            body,
            grid=(1,),
            out_shape=outs,
            in_specs=specs,
            out_specs=[held] * len(outs),
            scratch_shapes=list(scratch),
            compiler_params=pltpu.CompilerParams(vmem_limit_bytes=limit << 20),
            cost_estimate=cost,
        )(*args)

    sender, pool, medium_pool, slots, comp, member, fine_sender, centred, received, near, *faces = kernel(
        first_kernel,
        [
            shaped((16, D), BF16),
            shaped((16, D), BF16),
            shaped((128, D), F32),
            shaped((16, 64), jnp.int32),
            shaped((32, 1024), BF16),
            shaped((32, 128), BF16),
            shaped((1024, D), BF16),
            shaped((D, D), BF16),
            shaped((16, D), F32),
            shaped((1024, 8), jnp.int32),
        ]
        + [shaped((1, 128, D), BF16)] * 6,
        [far] * 13,
        (
            distant(fine_state), distant(row(fine_parent)), distant(medium_state), distant(row(medium_parent)),
            distant(coarse_state), distant(coarse_nbrs), distant(coarse_edge_in), distant(send_rows.reshape(1, 768)),
            distant(ghost_counts), distant(fine_edge_in), distant(fine_edge_out), distant(row(coarse_edge_bias)),
            distant(fine_nbrs.T),
        ),
        [
            pltpu.VMEM((1024, D), BF16),
            pltpu.VMEM((1, 1024), jnp.int32),
            pltpu.VMEM((128, D), BF16),
            pltpu.VMEM((1, 128), jnp.int32),
            pltpu.VMEM((16, D), BF16),
            pltpu.VMEM((16, 64), jnp.int32),
            pltpu.VMEM((D, D), BF16),
            pltpu.VMEM((1, 768), jnp.int32),
            pltpu.VMEM((D, D), BF16),
            pltpu.VMEM((D, D), BF16),
            pltpu.VMEM((D, D), BF16),
            pltpu.VMEM((6, 1024), jnp.int32),
            pltpu.SMEM((1, 6), jnp.int32),
            pltpu.VMEM((1, D), F32),
            pltpu.SemaphoreType.DMA((14,)),
        ],
    )

    def faced(face):
        axes = (("x", "zh", "c"), "y")[face // 2]
        count = lax.axis_size(axes)
        pairs = [(k, k + 1) for k in range(count - 1)]
        return lax.ppermute(faces[face], axes, [(b, a) for a, b in pairs] if face % 2 == 0 else pairs)

    low, high = sent(sender, UP_Z), sent(sender, DOWN_Z)
    low_y = faced(3)
    low, high, low_y, faces[0], faces[1] = tied((low, high, low_y, faces[0], faces[1]))
    three = joined(high, sender, low)
    lower, higher = sent(three, UP_3Z), sent(three[16:], DOWN_3Z)
    low_x, high_x = faced(1), faced(0)
    lower, higher, low_x, faces[2], faces[4], faces[5] = tied((lower, higher, low_x, faces[2], faces[4], faces[5]))
    column = joined(three, lower, higher)
    up, down = sent(column, UP_FIRST), sent(column, DOWN_FIRST)
    high_y = faced(2)
    low_z, high_z = sent(faces[5], UP_Z), sent(faces[4], DOWN_Z)
    near_faces = [low_x, high_x, low_y, high_y, low_z, high_z]
    (table,) = kernel(
        table_kernel,
        [shaped((1792, D), BF16)],
        [pl.BlockSpec(memory_space=pl.ANY)] * 7,
        (fine_sender, *near_faces),
        [pltpu.SemaphoreType.DMA((7,))],
    )
    news = []

    def edges(blocks):
        first = sum(new.shape[0] for new in news) // BLOCK
        news.extend(
            kernel(
                functools.partial(edge_kernel, first=first),
                [shaped((blocks * BLOCK, D), F32)],
                [held] * 3 + [upper] + [held] * 7,
                (
                    table, fine_state, near, fine_edge_in, row(fine_edge_bias), centred, row(fine_edge_gain),
                    fine_node_in, row(fine_node_bias), fine_node_out, row(fine_node_gain),
                ),
                [pltpu.VMEM((2, 6 * BLOCK, 1792), BF16), pltpu.VMEM((2, 6 * BLOCK, D), BF16)],
                cost=pl.CostEstimate(
                    flops=blocks * 1_700_000_000, bytes_accessed=blocks * 3_000_000, transcendentals=0
                ),
            )
        )

    rest = [sent(up[:64], UP_FIRST), sent(down[64:], DOWN_FIRST)]
    line = joined(column, up, down, *rest)
    table, line = tied((table, line))
    up, down = sent(line, UP_SECOND), sent(line, DOWN_SECOND)
    edges(SHARES[0])
    up, down, news[-1] = tied((up, down, news[-1]))
    table, up = tied((table, up))
    rest = [sent(up[:256], UP_SECOND), sent(down[256:], DOWN_SECOND)]
    edges(SHARES[1])
    line, up, down, *rest, news[-1] = tied((line, up, down, *rest, news[-1]))
    table, rest[0] = tied((table, rest[0]))
    others = [sent(part, SWAP) for part in (line, up, down, *rest)]
    edges(SHARES[2])
    (found,) = kernel(
        gather_kernel, [shaped((1024, D), BF16)], [held] * 6, (slots, line, up, down, *rest), limit=40,
        cost=pl.CostEstimate(flops=2_000_000_000, bytes_accessed=4_000_000, transcendentals=0),
    )
    fine_out, medium_out, coarse_out = kernel(
        coarse_kernel,
        [shaped((1024, D), BF16), shaped((128, D), BF16), shaped((16, D), BF16)],
        [held] * (18 + len(news)),
        (
            found, *others, slots, pool, medium_pool, comp, member, *news, received,
            coarse_edge_out, row(coarse_edge_gain), coarse_node_in, row(coarse_node_bias), coarse_node_out,
            row(coarse_node_gain),
        ),
        limit=48,
    )
    return fine_out, medium_out, coarse_out


def solution(mesh):
    torus = Mesh(mesh.devices.reshape(SIZES), AXES)
    rows = P(AXES, None)
    placed = (rows, rows, P(AXES, None, None), rows, P(AXES), rows, P(AXES), rows, rows) + (P(),) * 16
    return jax.shard_map(local, mesh=torus, in_specs=placed, out_specs=(rows, rows, rows), check_vma=False)
```
